32 devices in a mesh: section: 2 (over x), dp: 16 (over z, y, core).
Axes of the slice: x: 2, y: 2, z: 4, core: 2. Of those that a mesh axis runs over, the one named last changes fastest.
Arguments:
- block_ends: bfloat16 [2, 2, 16384, 1024], P('section', None, 'dp'), may hold values from -6 to 6
- proj_in: bfloat16 [2, 524288], P('section', 'dp'), may hold values from -0.1875 to 0.1875
- proj_out: bfloat16 [2, 524288], P('section', 'dp'), may hold values from -0.25 to 0.25
- conv_taps: bfloat16 [2, 4, 262144], P('section', None, 'dp'), may hold values from -0.125 to 0.125
- norm_gains: float32 [2, 2048], P('section'), may hold values from 0.1 to 1.9
- bias_terms: float32 [2, 3072], P('section'), may hold values from -2 to 2
- lengths: int32 [2, 16, 8], P(None, 'dp'), may hold values from 1 to 512, 1024 in all within a row
- dilation: int32 [2], replicated, may hold values from 1 to 64, as said below
Outputs:
- activations: bfloat16 [2, 2, 16384, 1024], P('section', None, 'dp')
- grads_io: float32 [2, 2, 16384, 1024], P('section', None, 'dp')
- grad_proj_in: float32 [2, 524288], P('section', 'dp')
- grad_proj_out: float32 [2, 524288], P('section', 'dp')
- grad_conv_taps: float32 [2, 4, 262144], P('section', None, 'dp')
- grad_norm_gains: float32 [2, 2048], P('section')
- grad_bias_terms: float32 [2, 3072], P('section')
The draws below stay inside these ranges and needn't reach their ends.
Inputs may be any that keep to these rules, and one draw needn't show every extreme that they name: Each sequence's 8 sentence lengths add up to 1024. `dilation`: the two dilations differ.
All inputs are finite; a program needn't handle non-finite values.
Results may differ from the reference program's by a relative error of at most 0.0096.
Values may be sent and summed in bfloat16 or wider, within the bound.
A program may use at most 256 MiB of HBM per device.

```python
import math
import jax
import jax.numpy as jnp
import numpy as np
from jax import lax

D = 1024
H = 512
LEN = 1024
MICRO = 2
SENT = 8
SEQS = 16
ROWS = 16384


def draw_dilation(key, part):
    key = jax.random.fold_in(key, 5)
    first_key, second_key = jax.random.split(key)
    widest_value = LEN // 16
    other = jax.random.randint(first_key, (), 1, widest_value, dtype=jnp.int32)
    widest = jax.random.randint(second_key, (), 0, 2, dtype=jnp.int32)
    return jnp.where(jnp.arange(2, dtype=jnp.int32) == widest, widest_value, other).astype(jnp.int32)


def level_of(key, dims, cuts, low, top_value):
    level, own = 1.0, jax.random.fold_in(key, 6)
    for dim, shards_of in cuts:
        draws = jnp.exp(jax.random.uniform(jax.random.fold_in(own, dim), (shards_of,), jnp.float32, low / len(cuts), top_value / len(cuts)))
        level = level * jnp.repeat(draws, dims[dim] // shards_of).reshape([-1 if axis == dim else 1 for axis in range(len(dims))])
    return level


def split_up(amount, total, reach, lean):
    portions = [(1 << 20) // math.isqrt(grade ** lean) + 1 for grade in range(2, amount + 1)]
    spare, counts = total - reach - (amount - 1), [1] * (amount - 1)
    while spare > 0:
        free = [i for i in range(amount - 1) if counts[i] < reach]
        mass, remaining = sum([portions[i] for i in free]), spare
        for i in free:
            extra = min(reach - counts[i], max(1, remaining * portions[i] // mass), spare)
            counts[i] = counts[i] + extra
            spare = spare - extra
    return np.array([reach] + counts)


def uneven(rng, number_of, total, limit, skew):
    if number_of == 2:
        one = jax.random.randint(rng, (), max(1, total - limit), min(limit, total - 1) + 1)
        return jnp.stack([one, total - one])
    tallies = jnp.asarray(split_up(number_of, total, limit, skew), jnp.int32)
    couples = (number_of - 1) // 2
    donor, taker = tallies[1:1 + 2 * couples:2], tallies[2:2 + 2 * couples:2]
    margin = jnp.minimum(donor - 1, limit - taker)
    shifted = jax.random.randint(jax.random.fold_in(rng, 1), (couples,), 0, 1 << 20) % (margin + 1)
    tallies = tallies.at[1:1 + 2 * couples:2].set(donor - shifted).at[2:2 + 2 * couples:2].set(taker + shifted)
    return tallies[jax.random.permutation(jax.random.fold_in(rng, 2), number_of)]


def gaussian(rng, dims, scale, limit, cuts=(), kind=jnp.bfloat16):
    array = jax.random.normal(rng, dims, jnp.float32) * scale
    if len(cuts) > 0:
        array = level_of(rng, dims, cuts, -0.22, 0.18) * array
    return jnp.clip(array, min=-limit, max=limit).astype(kind)


def setup_inputs(seed: int = 0) -> dict:
    key_list = jax.random.split(jax.random.key(seed), 9)
    block_ends = gaussian(key_list[0], (2, MICRO, ROWS, D), 1.0, 6.0, ((0, 2), (2, 16)))
    proj_in = gaussian(key_list[1], (2, D * H), D ** -0.5, 0.1875, ((0, 2), (1, 16)))
    proj_out = gaussian(key_list[2], (2, H * D), H ** -0.5, 0.25, ((0, 2), (1, 16)))
    conv_taps = gaussian(key_list[3], (2, 4, H * H), (4 * H) ** -0.5, 0.125, ((0, 2), (2, 16)))
    norm_gains = jnp.clip(1.0 + 0.18 * jax.random.normal(key_list[4], (2, D + 2 * H), jnp.float32), 0.1, 1.9)
    bias_terms = gaussian(key_list[5], (2, 2 * D + 2 * H), 0.3, 2.0, ((0, 2),), jnp.float32)
    lengths = jax.vmap(lambda own: uneven(own, SENT, LEN, LEN // 2, 1))(jax.random.split(key_list[6], MICRO * SEQS)).reshape((MICRO, SEQS, SENT)).astype(jnp.int32)
    dilation = draw_dilation(jax.random.fold_in(key_list[8], 71), 0)
    return dict(block_ends=block_ends, proj_in=proj_in, proj_out=proj_out, conv_taps=conv_taps, norm_gains=norm_gains, bias_terms=bias_terms, lengths=lengths, dilation=dilation)


@jax.custom_vjp
def low(v):
    return lax.optimization_barrier(v.astype(jnp.bfloat16)).astype(jnp.float32)

@jax.custom_vjp
def low_back(v):
    return v

def low_keep(v):
    return (low(v), None)

def low_pass(kept, grad):
    return (grad,)

def back_keep(v):
    return (v, None)

def back_low(kept, grad):
    return (low(grad),)
low.defvjp(low_keep, low_pass)
low_back.defvjp(back_keep, back_low)
epsilon = 1e-05

def norm_gelu(values, gain, shift_bias):
    centre = values - lax.optimization_barrier(jnp.mean(values, axis=-1, keepdims=True))
    spread = lax.optimization_barrier(jnp.mean(centre * centre, axis=-1, keepdims=True))
    return jax.nn.gelu(centre * lax.rsqrt(spread + epsilon) * gain + shift_bias)

def project(values, matrix):
    return jnp.einsum('abk,kn->abn', values, matrix, precision=lax.Precision.HIGHEST)

def tap_masks(sentence_lengths, offsets):
    seq_len = LEN
    bounds = jnp.cumsum(sentence_lengths, axis=-1, dtype=jnp.int32)
    position = jnp.arange(seq_len, dtype=jnp.int32)
    sentence = lax.optimization_barrier(jnp.sum((position[None, :, None] >= bounds[:, None, :]).astype(jnp.int32), axis=-1))
    result = []
    for offset in offsets:
        source = position + offset
        inside = (source >= 0) & (source < seq_len)
        partner = jnp.roll(sentence, -offset, axis=1)
        result.append((inside[None, :] & (partner == sentence)).astype(jnp.float32))
    return result

def residual_block(inputs, weight_in, weight_out, kernel, gains, biases, masks, offsets):
    a_first = low(norm_gelu(inputs, gains[:D], biases[:D]))
    hidden = low_back(project(a_first, weight_in))
    a_second = low(norm_gelu(hidden, gains[D:D + H], biases[2 * D:2 * D + H]))
    shifted_rows = jnp.concatenate([jnp.roll(a_second, -offset, axis=1) * tap_mask[:, :, None] for offset, tap_mask in zip(offsets, masks)], axis=-1)
    conv_out = low_back(project(shifted_rows, kernel.reshape(len(offsets) * H, H)))
    a_third = low(norm_gelu(conv_out, gains[D + H:], biases[2 * D + H:]))
    return inputs + project(a_third, weight_out) + biases[D:2 * D]

def reference(block_ends, proj_in, proj_out, conv_taps, norm_gains, bias_terms, lengths, dilation):
    seq_len = LEN
    total = MICRO * SEQS
    group = max(1, min(4096 // seq_len, total))
    while total % group:
        group -= 1
    steps_count = total // group
    inputs = block_ends[0].astype(jnp.float32).reshape(steps_count, group, seq_len, D)
    cotangent = block_ends[1].astype(jnp.float32).reshape(steps_count, group, seq_len, D)
    sentence_lengths = lengths.reshape(steps_count, group, SENT)
    params = (proj_in.astype(jnp.float32), proj_out.astype(jnp.float32), conv_taps.astype(jnp.float32), norm_gains.astype(jnp.float32), bias_terms.astype(jnp.float32))
    enc_offsets = [(tap_index - 2) * dilation[0] for tap_index in range(5)]
    dec_offsets = [(tap_index - 2) * dilation[1] for tap_index in range(3)]

    def forward(source, probe, weights, group_lengths):
        weight_in, weight_out, kernels, gains, biases = weights
        kernel_list = jnp.concatenate([kernels[0], kernels[1]], axis=0)
        encoded = residual_block(source, weight_in[0].reshape(D, H), weight_out[0].reshape(H, D), kernel_list[:5], gains[0], biases[0], tap_masks(group_lengths, enc_offsets), enc_offsets)
        passed = low_back(low(encoded)) + probe
        decoded = residual_block(passed, weight_in[1].reshape(D, H), weight_out[1].reshape(H, D), kernel_list[5:], gains[1], biases[1], tap_masks(group_lengths, dec_offsets), dec_offsets)
        return (decoded, encoded)

    def scan_step(carry, pieces):
        source, upstream, group_lengths = pieces

        def wrapped(first_arg, probe_arg, weight_arg):
            return forward(first_arg, probe_arg, weight_arg, group_lengths)
        decoded, pullback, encoded = jax.vjp(wrapped, source, jnp.zeros_like(source), params, has_aux=True)
        grad_source, grad_probe, grad_weights = pullback(upstream)
        carry = jax.tree.map(jnp.add, carry, grad_weights)
        return (carry, (encoded.astype(jnp.bfloat16), decoded.astype(jnp.bfloat16), grad_source, grad_probe))
    zero_grads = jax.tree.map(jnp.zeros_like, params)
    totals, outputs = lax.scan(scan_step, zero_grads, (inputs, cotangent, sentence_lengths))
    layout = (MICRO, SEQS * seq_len, D)
    activations = jnp.stack([outputs[0].reshape(layout), outputs[1].reshape(layout)])
    grads_io = jnp.stack([outputs[2].reshape(layout), outputs[3].reshape(layout)])
    return (activations, grads_io, totals[0], totals[1], totals[2], totals[3], totals[4])
```

```python
import functools

import jax
import jax.numpy as jnp
from jax import lax
from jax.experimental import pallas as pl
from jax.experimental.pallas import tpu as pltpu
from jax.sharding import Mesh
from jax.sharding import PartitionSpec as P

D = 1024
H = 512
LEN = 1024
POSITIONS = 16
RING = 8
TILE = 256
TILES = LEN // TILE
PAD = 128
LANES = 128
PANELS = H // LANES
epsilon = 1e-05
linear_term = 0.7978845608028654
cubic_term = linear_term * 0.044715
kappa = cubic_term ** (1.0 / 3.0)
beta = linear_term / kappa
MESH = pl.DeviceIdType.MESH
F32 = jnp.float32
BF16 = jnp.bfloat16

PIECE = 256
EARLY = ((0, 0, 96), (0, 96, 160), (1, 0, 32))
LATE = ((1, 32, 64), (1, 96, 160))
PARTS = EARLY + LATE
GRAD = 288
HALF = GRAD // 2
ACC_ROWS = 2 * D + 5 * H
STAT = 5 * D


def product(left, right):
    return jnp.dot(left, right, preferred_element_type=F32)


def contract_rows(left, right):
    return lax.dot_general(left, right, (((0,), (0,)), ((), ())), preferred_element_type=F32)


def contract_columns(left, right):
    return lax.dot_general(left, right, (((1,), (1,)), ((), ())), preferred_element_type=F32)


def normalise(values):
    mean = jnp.mean(values, axis=-1, keepdims=True)
    centre = values - mean
    scale = lax.rsqrt(jnp.mean(centre * centre, axis=-1, keepdims=True) + epsilon)
    return centre * scale, mean, scale


def gelu(normal, gain, bias):
    half = normal * (0.5 * gain) + 0.5 * bias
    inner = half * (half * half * (8.0 * cubic_term) + 2.0 * linear_term)
    return half + half * jnp.tanh(inner)


def gelu_norm_back(normal, scale, gain, bias, upstream):
    arg = normal * (kappa * gain) + kappa * bias
    square = arg * arg
    bend = jnp.tanh(arg * (square + beta))
    slope = arg * (3.0 * square + beta)
    double_q = upstream * ((1.0 + bend) * (1.0 + (1.0 - bend) * slope))
    weighted = (0.5 * gain) * double_q
    count = 1.0 / normal.shape[-1]
    mean = jnp.sum(weighted, axis=-1, keepdims=True) * count
    along = jnp.sum(weighted * normal, axis=-1, keepdims=True) * count
    return (weighted - mean - normal * along) * scale, double_q * normal, double_q


def fold_rows(values):
    return jnp.sum(values.reshape(values.shape[0] // 8, 8, values.shape[1]), axis=0)


def ring_chip(place):
    place = lax.rem(place + 2 * RING, RING)
    return jnp.where(place < RING // 2, 2 * place, 2 * (RING - place) - 1)


def kernel(group, dilation, lengths, ends, piece, params, *refs):
    (
        act_out,
        gio_out,
        grad_in_out,
        grad_out_out,
        grad_tap_out,
        gain_out,
        bias_out,
        weights,
        own,
        bufs,
        panels,
        a_first,
        a_second,
        a_third,
        stats,
        bounds,
        acc,
        vec,
        gio_stage,
        act_stage,
        vectors,
        sums,
        tap_send,
        tap_land,
        ring_send,
        ring_recv,
        sib_send,
        sib_recv,
        cross_send,
        cross_recv,
        raw_send,
        raw_recv,
        pass_send,
        pass_recv,
        local_sem,
        act_sem,
        gio_sem,
        red_send,
        red_recv,
        vec_send,
        vec_recv,
        tap_sem,
        ready,
    ) = refs
    section = lax.axis_index("section")
    index = lax.axis_index("dp")
    place, lane = index // group, lax.rem(index, group)
    chip, core = place // 2, lax.rem(place, 2)
    ring = jnp.where(lax.rem(chip, 2) == 0, chip // 2, RING - (chip + 1) // 2)

    def device(sec, position):
        return {"section": sec, "dp": position * group + lane}

    def position(ring_place, which_core):
        return 2 * ring_chip(ring_place) + which_core

    peer = device(1 - section, place)
    sibling = device(section, 2 * chip + 1 - core)
    after = device(section, position(ring + 1, core))
    before = device(section, position(ring - 1, core))

    def remote(src, dst, send, recv, target):
        return pltpu.make_async_remote_copy(
            src_ref=src, dst_ref=dst, send_sem=send, recv_sem=recv, device_id=target, device_id_type=MESH
        )

    barrier = pltpu.get_barrier_semaphore()
    for target in (peer, sibling, after, before):
        pl.semaphore_signal(barrier, inc=1, device_id=target, device_id_type=MESH)
    pl.semaphore_wait(barrier, 4)

    def rows_of(part, origin, half=None):
        sec, first, rows = PARTS[part]
        if half is not None:
            first, rows = first + half * (rows // 2), rows // 2
        return pl.ds(pl.multiple_of((sec * POSITIONS + origin) * PIECE + first, 16), rows)

    def ring_copy(part, hop, way):
        step = 1 if way == 0 else -1
        rows = rows_of(part, position(ring - step * (hop - 1), core), way if hop == 4 else None)
        return remote(
            weights.at[rows], weights.at[rows], ring_send.at[way, part, hop - 1], ring_recv.at[way, part, hop - 1],
            after if way == 0 else before,
        )

    def ring_arrival(part, hop, way):
        step = 1 if way == 0 else -1
        rows = rows_of(part, position(ring - step * hop, core), way if hop == 4 else None)
        return remote(
            weights.at[rows], weights.at[rows], ring_send.at[way, part, hop - 1], ring_recv.at[way, part, hop - 1],
            after if way == 0 else before,
        )

    def share_copy(part, ring_place, slot, which_core):
        rows = rows_of(part, position(ring_place, which_core))
        return remote(
            weights.at[rows], weights.at[rows], sib_send.at[part, slot], sib_recv.at[part, slot], sibling
        )

    def start_part(part):
        for way in range(2):
            ring_copy(part, 1, way).start()
        share_copy(part, ring, 0, core).start()

    def advance(part, hop):
        for way in range(2):
            ring_arrival(part, hop, way).wait_recv()
            if hop < 4:
                ring_copy(part, hop + 1, way).start()
                share_copy(part, ring - hop if way == 0 else ring + hop, 2 * hop - 1 + way, core).start()
        if hop == 4:
            share_copy(part, ring + 4, 7, core).start()

    def wait_shared(parts):
        for part in parts:
            share_copy(part, ring, 0, 1 - core).wait_recv()
            for hop in range(1, 4):
                for way in range(2):
                    share_copy(part, ring - hop if way == 0 else ring + hop, 2 * hop - 1 + way, 1 - core).wait_recv()
            share_copy(part, ring + 4, 7, 1 - core).wait_recv()

    def cross_copy(half, sec):
        first, rows = ((0, 96), (96, 160))[half]
        slot = pl.ds(pl.multiple_of((sec * POSITIONS + place) * PIECE + first, 16), rows)
        return remote(piece.at[pl.ds(first, rows)], weights.at[slot], cross_send.at[half], cross_recv.at[half], peer)

    def cross_params(sec):
        return remote(params, vectors.at[sec], cross_send.at[2], cross_recv.at[2], peer)

    def tile_rows(t):
        return pl.ds(pl.multiple_of(t * TILE, TILE), TILE)

    def raw_copy(t):
        return remote(
            ends.at[section, tile_rows(t)], bufs.at[2, tile_rows(t)], raw_send.at[t], raw_recv.at[t], peer
        )

    for half in range(2):
        cross_copy(half, section).start()
    cross_params(section).start()
    for t in range(TILES):
        raw_copy(t).start()
    own_slot = pl.ds(pl.multiple_of((section * POSITIONS + place) * PIECE, PIECE), PIECE)
    keep_piece = pltpu.make_async_copy(piece, weights.at[own_slot], local_sem.at[0])
    keep_params = pltpu.make_async_copy(params, vectors.at[section], local_sem.at[1])
    keep_ends = pltpu.make_async_copy(ends, own, local_sem.at[2])
    keep_piece.start()
    keep_params.start()
    keep_ends.start()
    keep_piece.wait()

    @pl.when(section == 0)
    def _():
        start_part(0)
        start_part(1)

    @pl.when(section == 1)
    def _():
        start_part(2)

    acc[...] = jnp.zeros_like(acc)
    vec[...] = jnp.zeros_like(vec)
    for half in range(2):
        cross_copy(half, 1 - section).wait_recv()

    @pl.when(section == 0)
    def _():
        start_part(2)

    @pl.when(section == 1)
    def _():
        start_part(0)
        start_part(1)

    for hop in range(1, 5):
        for part in range(3):
            advance(part, hop)
        if hop == 3:
            for part in range(3, 5):
                start_part(part)
    wait_shared(range(3))
    keep_params.wait()
    keep_ends.wait()
    cross_params(1 - section).wait_recv()

    def advance_late(hop):
        for part in range(3, 5):
            advance(part, hop)
        if hop == 4:
            wait_shared(range(3, 5))

    def matrix(sec, first, rows):
        starts = [(sec * POSITIONS + pos) * PIECE + first for pos in range(POSITIONS)]
        return jnp.concatenate([weights[start : start + rows, :] for start in starts], axis=0)

    def weight_in(block):
        return matrix(block, 32, 64)

    def weight_out(block, half):
        return matrix(block, 96 + 32 * half, 32)

    def tap(block, k):
        sec, slot = (0, k) if block == 0 and k < 4 else (1, 0) if block == 0 else (1, k + 1)
        return matrix(sec, 0 if slot == 0 else 128 + 32 * slot, 32)

    def gain(block, norm):
        first, size = ((0, D), (D, H), (D + H, H))[norm]
        return vectors[block, :, first : first + size]

    def bias(block, norm):
        first, size = ((0, D), (2 * D, H), (2 * D + H, H))[norm]
        return vectors[block, :, 2 * D + first : 2 * D + first + size]

    def out_bias(block, half):
        first = 3 * D + half * H
        return vectors[block, :, first : first + H]

    def put_panels(which, base, values):
        for j in range(PANELS):
            panels[which, j, pl.ds(PAD + base, TILE), :] = values[:, j * LANES : (j + 1) * LANES]

    def get_panels(which, start):
        return jnp.concatenate([panels[which, j, pl.ds(start, TILE), :] for j in range(PANELS)], axis=1)

    def shifted(which, base, offset):
        values = get_panels(which, PAD + base + offset)
        inside = (bounds[0, pl.ds(base, TILE), :] <= offset) & (bounds[1, pl.ds(base, TILE), :] > offset)
        return jnp.where(jnp.concatenate([inside] * PANELS, axis=1), values, 0.0).astype(BF16)

    def sentence_bounds(m):
        row = lax.broadcasted_iota(jnp.int32, (LEN, LANES), 0)
        first = jnp.zeros((LEN, LANES), jnp.int32)
        last = jnp.full((LEN, LANES), LEN, jnp.int32)
        reached = jnp.int32(0)
        for j in range(8):
            end = reached + lengths[m, j]
            inside = (row >= reached) & (row < end)
            first = jnp.where(inside, reached, first)
            last = jnp.where(inside, end, last)
            reached = end
        bounds[0] = first - row
        bounds[1] = last - row

    taps = (5, 3)

    def add_rows(first, rows, values):
        acc[pl.ds(first, rows), :] += values

    def forward_in(block, source, t, shift_panel, keep_panel, keep_act):
        base = pl.multiple_of(t * TILE, TILE)
        rows = pl.ds(base, TILE)
        normal, mean, scale = normalise(source[rows, :].astype(F32))
        act = gelu(normal, gain(block, 0), bias(block, 0)).astype(BF16)
        if keep_panel is not None:
            stats[block, 0, rows, :] = mean
            stats[block, 1, rows, :] = scale
        if keep_act:
            a_first[rows, :] = act
        normal, _, scale = normalise(product(act, weight_in(block)))
        act = gelu(normal, gain(block, 1), bias(block, 1)).astype(BF16)
        if keep_panel is not None:
            stats[block, 2, rows, :] = scale
            put_panels(keep_panel, base, normal)
        if keep_act:
            a_second[rows, :] = act
        put_panels(shift_panel, base, act.astype(F32))

    def forward_out(block, source, t, shift_panel, keep_panel, keep_act, store):
        base = pl.multiple_of(t * TILE, TILE)
        rows = pl.ds(base, TILE)
        conv = None
        for k in range(taps[block]):
            term = product(shifted(shift_panel, base, (k - 2) * dilation[block]), tap(block, k))
            conv = term if conv is None else conv + term
        normal, _, scale = normalise(conv)
        if keep_panel is not None:
            stats[block, 3, rows, :] = scale
            put_panels(keep_panel, base, normal)
        if store is None:
            return
        act = gelu(normal, gain(block, 2), bias(block, 2)).astype(BF16)
        if keep_act:
            a_third[rows, :] = act
        for half in range(2):
            cols = slice(half * H, (half + 1) * H)
            residual = source[rows, cols].astype(F32) + product(act, weight_out(block, half))
            store(cols, (residual + out_bias(block, half)).astype(BF16))

    def backward_out(block, grad, t, panel, with_grads):
        base = pl.multiple_of(t * TILE, TILE)
        rows = pl.ds(base, TILE)
        upstream = contract_columns(grad[rows, 0:H], weight_out(block, 0))
        upstream = upstream + contract_columns(grad[rows, H:D], weight_out(block, 1))
        back, double_qn, double_q = gelu_norm_back(
            get_panels(panel, PAD + base), stats[block, 3, rows, :], gain(block, 2), bias(block, 2), upstream
        )
        if with_grads:
            vec[0, :, D + H : 2 * D] += fold_rows(double_qn)
            vec[1, :, D + H : 2 * D] += fold_rows(double_q)
            vec[2, :, 0:D] += fold_rows(grad[rows, :].astype(F32))
            act = a_third[rows, :]
            for half in range(2):
                add_rows(D + half * H, H, contract_rows(act, grad[rows, half * H : (half + 1) * H]))
        put_panels(panel, base, back.astype(BF16).astype(F32))

    def backward_in(block, source, grad, t, panel, normal_panel, with_grads, store):
        base = pl.multiple_of(t * TILE, TILE)
        rows = pl.ds(base, TILE)
        upstream = None
        for k in range(taps[block]):
            moved = shifted(panel, base, (2 - k) * dilation[block])
            term = contract_columns(moved, tap(block, k))
            upstream = term if upstream is None else upstream + term
            if with_grads:
                slot = k if block == 0 else k + 1
                add_rows(2 * D + slot * H, H, contract_rows(a_second[rows, :], moved))
        back, double_qn, double_q = gelu_norm_back(
            get_panels(normal_panel, PAD + base), stats[block, 2, rows, :], gain(block, 1), bias(block, 1), upstream
        )
        back = back.astype(BF16)
        if with_grads:
            vec[0, :, D : D + H] += fold_rows(double_qn)
            vec[1, :, D : D + H] += fold_rows(double_q)
            add_rows(0, D, contract_rows(a_first[rows, :], back))
        upstream = contract_columns(back, weight_in(block))
        scale = stats[block, 1, rows, :]
        normal = (source[rows, :].astype(F32) - stats[block, 0, rows, :]) * scale
        back, double_qn, double_q = gelu_norm_back(normal, scale, gain(block, 0), bias(block, 0), upstream)
        if with_grads:
            vec[0, :, 0:D] += fold_rows(double_qn)
            vec[1, :, 0:D] += fold_rows(double_q)
        store(grad[rows, :].astype(F32) + back)

    def act_copy(m, t, staged):
        src = act_stage.at[lax.rem(t, 2)] if staged else bufs.at[0, tile_rows(t)]
        return pltpu.make_async_copy(src, act_out.at[m, tile_rows(t)], act_sem.at[lax.rem(t, 2)])

    def gio_copy(m, t):
        slot = lax.rem(t, 2)
        return pltpu.make_async_copy(gio_stage.at[slot], gio_out.at[m, tile_rows(t)], gio_sem.at[slot])

    def act_pass(t):
        return remote(
            act_out.at[1, tile_rows(t)], bufs.at[1, tile_rows(t)], pass_send.at[t], pass_recv.at[t], peer
        )

    def grad_pass(t):
        return remote(bufs.at[2, tile_rows(t)], bufs.at[1, tile_rows(t)], pass_send.at[t], pass_recv.at[t], peer)

    def settle(copy, t, count):
        @pl.when(t >= 1)
        def _():
            copy(t - 1).wait()

        @pl.when(t == count - 1)
        def _():
            copy(t).wait()

    @pl.when(section == 0)
    def _():
        @pl.loop(0, 2)
        def _(i):
            m = 1 - i
            source = own.at[m]
            sentence_bounds(m)

            @pl.loop(0, TILES + 1)
            def _(t):
                @pl.when(t < TILES)
                def _():
                    forward_in(0, source, t, 4, 0, True)

                @pl.when(t >= 1)
                def _():
                    done = t - 1

                    def store(cols, values):
                        bufs[0, tile_rows(done), cols] = values

                    forward_out(0, source, done, 4, 1, True, store)
                    act_copy(m, done, False).start()
                    settle(lambda s: act_copy(m, s, False), done, TILES)

                for hop in range(1, 5):

                    @pl.when((i == 0) & (t == hop))
                    def _():
                        advance_late(hop)

            @pl.when(i == 0)
            def _():
                for t in range(TILES):
                    act_pass(t).start()

                @pl.loop(0, TILES + 1)
                def _(t):
                    @pl.when(t < TILES)
                    def _():
                        raw_copy(t).wait_recv()
                        forward_in(1, bufs.at[0], t, 4, 2, False)
                        forward_out(1, bufs.at[0], t, 4, 3, False, None)
                        backward_out(1, bufs.at[2], t, 3, False)

                    @pl.when(t >= 1)
                    def _():
                        done = t - 1

                        def store(values):
                            bufs[2, tile_rows(done), :] = values.astype(BF16)

                        backward_in(1, bufs.at[0], bufs.at[2], done, 3, 2, False, store)

            grad = bufs.at[2 - i]

            @pl.loop(0, TILES + 1)
            def _(t):
                @pl.when((t < TILES) & (i == 1))
                def _():
                    grad_pass(t).wait_recv()

                @pl.when(t < TILES)
                def _():
                    backward_out(0, grad, t, 1, True)

                @pl.when(t >= 1)
                def _():
                    done = t - 1

                    def store(values):
                        gio_stage[lax.rem(done, 2)] = values

                    backward_in(0, source, grad, done, 1, 0, True, store)
                    gio_copy(m, done).start()
                    settle(lambda s: gio_copy(m, s), done, TILES)

        for t in range(TILES):
            act_pass(t).wait_send()

    @pl.when(section == 1)
    def _():
        @pl.loop(0, 2)
        def _(i):
            sentence_bounds(i)
            source = bufs.at[i]
            grad = own.at[i]

            @pl.loop(0, TILES + 2)
            def _(t):
                @pl.when((i == 0) & (t < TILES))
                def _():
                    raw_copy(t).wait_recv()
                    forward_in(0, bufs.at[2], t, 0, None, False)

                @pl.when((i == 0) & (t >= 1) & (t <= TILES))
                def _():
                    done = t - 1

                    def store(cols, values):
                        bufs[0, tile_rows(done), cols] = values

                    forward_out(0, bufs.at[2], done, 0, None, False, store)

                @pl.when((i == 0) & (t == 0))
                def _():
                    advance_late(1)

                @pl.when((i == 0) & (t == 1))
                def _():
                    for hop in range(2, 5):
                        advance_late(hop)

                @pl.when((i == 1) & (t >= 1) & (t <= TILES))
                def _():
                    act_pass(t - 1).wait_recv()

                @pl.when((t >= 1) & (t <= TILES))
                def _():
                    done = t - 1

                    def store(cols, values):
                        act_stage[lax.rem(done, 2), :, cols] = values

                    forward_in(1, source, done, 4, 2, True)
                    forward_out(1, source, done, 4, 3, True, store)
                    act_copy(i, done, True).start()
                    settle(lambda s: act_copy(i, s, True), done, TILES)
                    backward_out(1, grad, done, 3, True)

                @pl.when(t >= 2)
                def _():
                    done = t - 2

                    def store(values):
                        gio_stage[lax.rem(done, 2)] = values

                        @pl.when(i == 0)
                        def _():
                            bufs[2, tile_rows(done), :] = values.astype(BF16)

                    backward_in(1, source, grad, done, 3, 2, True, store)

                    @pl.when(i == 0)
                    def _():
                        grad_pass(done).start()

                    gio_copy(i, done).start()
                    settle(lambda s: gio_copy(i, s), done, TILES)

        for t in range(TILES):
            grad_pass(t).wait_send()

    for part in range(5):
        for hop in range(1, 5):
            for way in range(2):
                ring_copy(part, hop, way).wait_send()
        share_copy(part, ring, 0, core).wait_send()
        for slot in range(1, 8):
            share_copy(part, ring, slot, core).wait_send()
    for half in range(2):
        cross_copy(half, section).wait_send()
    cross_params(section).wait_send()
    for t in range(TILES):
        raw_copy(t).wait_send()

    for target in (sibling, after, before):
        pl.semaphore_signal(ready, inc=1, device_id=target, device_id_type=MESH)
    pl.semaphore_wait(ready, 3)

    def grad_rows(pos):
        found = [(64 * pos, 64, 0), (D + 32 * pos, 32, 64), (D + H + 32 * pos, 32, 96)]
        for number, slot in enumerate((1, 2, 3, 0, 4)):
            found.append((2 * D + slot * H + 32 * pos, 32, 128 + 32 * number))
        return found

    def own_piece(pos):
        return jnp.concatenate(
            [acc[pl.ds(pl.multiple_of(first, 32), rows), :] for first, rows, _ in grad_rows(pos)], axis=0
        )

    sib_out = 0
    sib_land = RING * GRAD
    ring_land = 2 * RING * GRAD
    ring_stage = ring_land + 8 * GRAD

    def sib_copy(slot):
        src = weights.at[pl.ds(sib_out + slot * GRAD, GRAD)]
        dst = weights.at[pl.ds(sib_land + slot * GRAD, GRAD)]
        return remote(src, dst, red_send.at[2, slot], red_recv.at[2, slot], sibling)

    order = (4, 3, 5, 2, 6, 1, 7, 0)
    for slot in order:
        weights[pl.ds(sib_out + slot * GRAD, GRAD), :] = own_piece(position(ring + slot, 1 - core)).astype(BF16)
        sib_copy(slot).start()

    line = jnp.concatenate(
        [
            0.5 * jnp.sum(vec[0], axis=0, keepdims=True),
            0.5 * jnp.sum(vec[1, :, 0:D], axis=0, keepdims=True),
            jnp.sum(vec[2, :, 0:D], axis=0, keepdims=True),
            0.5 * jnp.sum(vec[1, :, D : 2 * D], axis=0, keepdims=True),
        ],
        axis=1,
    )
    for row in range(8):
        sums[0, row : row + 1, :] = line[:, row * 640 : (row + 1) * 640]

    def vec_share():
        return remote(sums.at[0], sums.at[1], vec_send.at[0], vec_recv.at[0], sibling)

    vec_share().start()

    def red_copy(way, step):
        rows = HALF if step == 1 else GRAD
        src = weights.at[pl.ds(ring_stage + (2 * way + step % 2) * GRAD, rows)]
        dst = weights.at[pl.ds(ring_land + (4 * way + step - 1) * GRAD, rows)]
        return remote(src, dst, red_send.at[way, step - 1], red_recv.at[way, step - 1], after if way == 0 else before)

    def both_cores(slot):
        pos = position(ring + slot, core)
        return own_piece(pos) + weights[pl.ds(sib_land + slot * GRAD, GRAD), :].astype(F32)

    def arrived(way, step):
        first = ring_land + (4 * way + step - 1) * GRAD
        if step == 1:
            half = weights[pl.ds(first, HALF), :].astype(F32)
            blank = jnp.zeros((HALF, H), F32)
            return jnp.concatenate([half, blank] if way == 0 else [blank, half], axis=0)
        return weights[pl.ds(first, GRAD), :].astype(F32)

    def vec_copy(way, hop):
        step = 1 if way == 0 else -1
        src = sums.at[2 + lax.rem(ring - step * (hop - 1) + 2 * RING, RING)]
        number = 1 + 4 * way + hop - 1
        return remote(src, src, vec_send.at[number], vec_recv.at[number], after if way == 0 else before)

    def vec_arrival(way, hop):
        step = 1 if way == 0 else -1
        dst = sums.at[2 + lax.rem(ring - step * hop + 2 * RING, RING)]
        number = 1 + 4 * way + hop - 1
        return remote(dst, dst, vec_send.at[number], vec_recv.at[number], after if way == 0 else before)

    sib_copy(4).wait_recv()
    farthest = both_cores(4).astype(BF16)
    for way in range(2):
        rows = pl.ds(ring_stage + (2 * way + 1) * GRAD, HALF)
        weights[rows, :] = farthest[0:HALF] if way == 0 else farthest[HALF:GRAD]
        red_copy(way, 1).start()
    vec_share().wait_recv()
    sums[2 + ring] = sums[0] + sums[1]
    for way in range(2):
        vec_copy(way, 1).start()
    for step in range(2, 5):
        for way in range(2):
            slot = 5 - step if way == 0 else 3 + step
            sib_copy(slot).wait_recv()
            red_copy(way, step - 1).wait_recv()
            total = both_cores(slot) + arrived(way, step - 1)
            if step > 2:
                red_copy(way, step - 2).wait_send()
            weights[pl.ds(ring_stage + (2 * way + step % 2) * GRAD, GRAD), :] = total.astype(BF16)
            red_copy(way, step).start()
        for way in range(2):
            vec_arrival(way, step - 1).wait_recv()
            if step < 4 or way == 0:
                vec_copy(way, step).start()
    sib_copy(0).wait_recv()
    total = both_cores(0)
    for way in range(2):
        red_copy(way, 4).wait_recv()
        total = total + arrived(way, 4)
    grad_in_out[...] = total[0:64]
    grad_out_out[0] = total[64:96]
    grad_out_out[1] = total[96:128]
    for slot in range(1, 4):
        grad_tap_out[slot] = total[96 + 32 * slot : 128 + 32 * slot]

    fifth = remote(tap_send, tap_land, tap_sem.at[0], tap_sem.at[1], peer)

    @pl.when(section == 0)
    def _():
        grad_tap_out[0] = total[224:256]
        tap_send[...] = total[256:288].astype(BF16)
        fifth.start()
        fifth.wait_send()

    vec_arrival(0, 4).wait_recv()
    line = sums[2]
    for chip_sum in range(1, RING):
        line = line + sums[2 + chip_sum]
    flat = jnp.concatenate([line[row : row + 1, :] for row in range(8)], axis=1)
    gain_out[...] = flat[:, 0 : 2 * D]
    bias_out[...] = flat[:, 2 * D : 5 * D]

    @pl.when(section == 1)
    def _():
        fifth.wait_recv()
        grad_tap_out[0] = tap_land[...].astype(F32)

    for way in range(2):
        for step in (3, 4):
            red_copy(way, step).wait_send()
        for hop in range(1, 5 if way == 0 else 4):
            vec_copy(way, hop).wait_send()
    for slot in range(RING):
        sib_copy(slot).wait_send()
    vec_share().wait_send()


def local(group, block_ends, proj_in, proj_out, conv_taps, norm_gains, bias_terms, lengths, dilation):
    micro, rows = block_ends.shape[1:3]
    if group > 1:
        proj_in = lax.all_gather(proj_in, "lane", axis=1, tiled=True)
        proj_out = lax.all_gather(proj_out, "lane", axis=1, tiled=True)
        conv_taps = lax.all_gather(conv_taps, "lane", axis=2, tiled=True)
    slots = conv_taps.reshape(4, 32, H)
    halves = proj_out.reshape(32, 2, H)
    piece = jnp.concatenate([slots[0], proj_in.reshape(64, H), halves[:, 0], halves[:, 1], slots[1], slots[2], slots[3]])
    params = jnp.concatenate([norm_gains, bias_terms], axis=1)
    vmem = pl.BlockSpec(memory_space=pltpu.VMEM)
    smem = pl.BlockSpec(memory_space=pltpu.SMEM)
    hbm = pl.BlockSpec(memory_space=pl.ANY)
    shape = jax.ShapeDtypeStruct
    dma = pltpu.SemaphoreType.DMA
    act, gio, grad_in, grad_out, grad_tap, gain_sum, bias_sum = pl.pallas_call(
        functools.partial(kernel, group),
        out_shape=[
            shape((micro, rows, D), BF16),
            shape((micro, rows, D), F32),
            shape((64, H), F32),
            shape((2, 32, H), F32),
            shape((4, 32, H), F32),
            shape((1, 2 * D), F32),
            shape((1, 3 * D), F32),
        ],
        in_specs=[smem, smem, hbm, vmem, vmem],
        out_specs=[hbm, hbm, vmem, vmem, vmem, vmem, vmem],
        scratch_shapes=[
            pltpu.VMEM((2 * POSITIONS * PIECE, H), BF16),
            pltpu.VMEM((micro, rows, D), BF16),
            pltpu.VMEM((3, LEN, D), BF16),
            pltpu.VMEM((5, PANELS, LEN + 2 * PAD, LANES), F32),
            pltpu.VMEM((LEN, D), BF16),
            pltpu.VMEM((LEN, H), BF16),
            pltpu.VMEM((LEN, H), BF16),
            pltpu.VMEM((2, 4, LEN, 1), F32),
            pltpu.VMEM((2, LEN, LANES), jnp.int32),
            pltpu.VMEM((ACC_ROWS, H), F32),
            pltpu.VMEM((3, 8, 2 * D), F32),
            pltpu.VMEM((2, TILE, D), F32),
            pltpu.VMEM((2, TILE, D), BF16),
            pltpu.VMEM((2, 1, STAT), F32),
            pltpu.VMEM((2 + RING, 8, 640), F32),
            pltpu.VMEM((32, H), BF16),
            pltpu.VMEM((32, H), BF16),
            dma((2, 5, 4)),
            dma((2, 5, 4)),
            dma((5, 8)),
            dma((5, 8)),
            dma((3,)),
            dma((3,)),
            dma((TILES,)),
            dma((TILES,)),
            dma((TILES,)),
            dma((TILES,)),
            dma((3,)),
            dma((2,)),
            dma((2,)),
            dma((3, 8)),
            dma((3, 8)),
            dma((9,)),
            dma((9,)),
            dma((2,)),
            pltpu.SemaphoreType.REGULAR,
        ],
        compiler_params=pltpu.CompilerParams(
            collective_id=0, has_side_effects=True, vmem_limit_bytes=64 << 20
        ),
        name="residual_blocks",
    )(dilation, lengths[:, 0, :], block_ends[0], piece, params)
    flat_out = jnp.stack([grad_out[0], grad_out[1]], axis=1)
    grads = (grad_in.reshape(1, -1), flat_out.reshape(1, -1), grad_tap.reshape(1, 4, -1))
    if group > 1:
        grads = tuple(
            lax.psum_scatter(part, "lane", scatter_dimension=part.ndim - 1, tiled=True) for part in grads
        )
        gain_sum, bias_sum = lax.psum((gain_sum, bias_sum), "lane")
    return (act[None], gio[None], *grads, gain_sum, bias_sum)


def solution(mesh):
    group = mesh.shape["dp"] // POSITIONS
    spread = "dp"
    if group > 1:
        mesh = Mesh(mesh.devices.reshape(2, POSITIONS, group), ("section", "dp", "lane"))
        spread = ("dp", "lane")
    placed = (
        P("section", None, spread, None),
        P("section", spread),
        P("section", spread),
        P("section", None, spread),
        P("section", None),
        P("section", None),
        P(None, spread, None),
        P(),
    )
    return jax.shard_map(
        functools.partial(local, group),
        mesh=mesh,
        in_specs=placed,
        out_specs=(
            P("section", None, spread, None),
            P("section", None, spread, None),
            P("section", spread),
            P("section", spread),
            P("section", None, spread),
            P("section", None),
            P("section", None),
        ),
        check_vma=False,
    )
```

```python
import functools

import jax
import jax.numpy as jnp
from jax import lax
from jax.experimental import pallas as pl
from jax.experimental.pallas import tpu as pltpu
from jax.sharding import Mesh
from jax.sharding import PartitionSpec as P

D = 1024
H = 512
LEN = 1024
POSITIONS = 16
RING = 8
TILE = 256
TILES = LEN // TILE
PAD = 128
CHUNK = 256
LANES = 128
PANELS = H // LANES
epsilon = 1e-05
linear_term = 0.7978845608028654
cubic_term = linear_term * 0.044715
kappa = cubic_term ** (1.0 / 3.0)
beta = linear_term / kappa
MESH = pl.DeviceIdType.MESH
F32 = jnp.float32
BF16 = jnp.bfloat16

PIECE = 256
EARLY = ((0, 0, 96), (0, 96, 160), (1, 0, 32))
LATE = ((1, 32, 64), (1, 96, 160))
PARTS = EARLY + LATE
TAPS = (5, 3)
ACC_BASE = (0, 2 * D + 5 * H)
ACC_ROWS = 4 * D + 8 * H
BATCHES = (
    (1, ((0, 64), (D, 32), (D + H, 32))),
    (1, ((2 * D, 32), (2 * D + H, 32), (2 * D + 2 * H, 32))),
    (0, ((D, 32), (D + H, 32), (2 * D + H, 32), (2 * D + 2 * H, 32))),
    (0, ((0, 64), (2 * D + 3 * H, 32), (2 * D, 32), (2 * D + 4 * H, 32))),
)
BATCH_ROWS = (128, 96, 128, 160)
SLOT_ROW = (0, 128, 0, 128)
REDUCED_ROW = (0, 128, 224, 352)
REDUCED = 512
MOST = 288
LEAD = 384


def product(left, right):
    return jnp.dot(left, right, preferred_element_type=F32)


def contract_rows(left, right):
    return lax.dot_general(left, right, (((0,), (0,)), ((), ())), preferred_element_type=F32)


def contract_columns(left, right):
    return lax.dot_general(left, right, (((1,), (1,)), ((), ())), preferred_element_type=F32)


def normalise(values):
    mean = jnp.mean(values, axis=-1, keepdims=True)
    centre = values - mean
    scale = lax.rsqrt(jnp.mean(centre * centre, axis=-1, keepdims=True) + epsilon)
    return centre * scale, mean, scale


def gelu(normal, gain, bias):
    half = normal * (0.5 * gain) + 0.5 * bias
    inner = half * (half * half * (8.0 * cubic_term) + 2.0 * linear_term)
    return half + half * jnp.tanh(inner)


def gelu_parts(normal, gain, bias):
    arg = normal * (kappa * gain) + kappa * bias
    square = arg * arg
    rise = 1.0 + jnp.tanh(arg * (square + beta))
    double_slope = rise * (1.0 + (2.0 - rise) * (arg * (3.0 * square + beta)))
    return arg, rise, double_slope


def gelu_again(arg, rise):
    return (arg * rise * (0.5 / kappa)).astype(BF16)


def norm_back(normal, scale, gain, double_q):
    weighted = (0.5 * gain) * double_q
    count = 1.0 / normal.shape[-1]
    mean = jnp.sum(weighted, axis=-1, keepdims=True) * count
    along = jnp.sum(weighted * normal, axis=-1, keepdims=True) * count
    return (weighted - mean - normal * along) * scale


def fold_rows(values):
    return jnp.sum(values.reshape(values.shape[0] // 8, 8, values.shape[1]), axis=0)


def ring_chip(place):
    place = lax.rem(place + 2 * RING, RING)
    return jnp.where(place < RING // 2, 2 * place, 2 * (RING - place) - 1)


def kernel(group, dilation, lengths, ends, proj_in, proj_out, conv_taps, gains, biases, *refs):
    (
        act_out,
        gio_out,
        grads_out,
        line_out,
        weights,
        own,
        bufs,
        panels,
        shift,
        stats,
        bounds,
        acc,
        vec,
        gio_stage,
        act_stage,
        all_gains,
        all_biases,
        sums,
        red,
        reduced,
        cross_out,
        cross_in,
        piece,
        middle,
        ring_send,
        ring_recv,
        sib_send,
        sib_recv,
        cross_send,
        cross_recv,
        raw_send,
        raw_recv,
        pass_send,
        pass_recv,
        local_sem,
        act_sem,
        gio_sem,
        red_send,
        red_recv,
        pair_send,
        pair_recv,
        vec_send,
        vec_recv,
        last_send,
        last_recv,
        ready,
    ) = refs
    section = lax.axis_index("section")
    index = lax.axis_index("dp")
    place, lane = index // group, lax.rem(index, group)
    chip, core = place // 2, lax.rem(place, 2)
    ring = jnp.where(lax.rem(chip, 2) == 0, chip // 2, RING - (chip + 1) // 2)

    def device(sec, position):
        return {"section": sec, "dp": position * group + lane}

    def position(ring_place, which_core):
        return 2 * ring_chip(ring_place) + which_core

    peer = device(1 - section, place)
    sibling = device(section, 2 * chip + 1 - core)
    after = device(section, position(ring + 1, core))
    before = device(section, position(ring - 1, core))

    def remote(src, dst, send, recv, target):
        return pltpu.make_async_remote_copy(
            src_ref=src, dst_ref=dst, send_sem=send, recv_sem=recv, device_id=target, device_id_type=MESH
        )

    barrier = pltpu.get_barrier_semaphore()
    for target in (peer, sibling, after, before):
        pl.semaphore_signal(barrier, inc=1, device_id=target, device_id_type=MESH)
    pl.semaphore_wait(barrier, 4)

    def rows_of(part, origin, half=None):
        sec, first, rows = PARTS[part]
        if half is not None:
            first, rows = first + half * (rows // 2), rows // 2
        return pl.ds(pl.multiple_of((sec * POSITIONS + origin) * PIECE + first, 16), rows)

    def ring_copy(part, hop, way):
        step = 1 if way == 0 else -1
        rows = rows_of(part, position(ring - step * (hop - 1), core), way if hop == 4 else None)
        return remote(
            weights.at[rows], weights.at[rows], ring_send.at[way, part, hop - 1], ring_recv.at[way, part, hop - 1],
            after if way == 0 else before,
        )

    def ring_arrival(part, hop, way):
        step = 1 if way == 0 else -1
        rows = rows_of(part, position(ring - step * hop, core), way if hop == 4 else None)
        return remote(
            weights.at[rows], weights.at[rows], ring_send.at[way, part, hop - 1], ring_recv.at[way, part, hop - 1],
            after if way == 0 else before,
        )

    def share_copy(part, ring_place, slot, which_core):
        rows = rows_of(part, position(ring_place, which_core))
        return remote(
            weights.at[rows], weights.at[rows], sib_send.at[part, slot], sib_recv.at[part, slot], sibling
        )

    def start_part(part):
        for way in range(2):
            ring_copy(part, 1, way).start()
        share_copy(part, ring, 0, core).start()

    def advance(part, hop):
        for way in range(2):
            ring_arrival(part, hop, way).wait_recv()
            if hop < 4:
                ring_copy(part, hop + 1, way).start()
                share_copy(part, ring - hop if way == 0 else ring + hop, 2 * hop - 1 + way, core).start()
        if hop == 4:
            share_copy(part, ring + 4, 7, core).start()

    def wait_shared(parts):
        for part in parts:
            share_copy(part, ring, 0, 1 - core).wait_recv()
            for hop in range(1, 4):
                for way in range(2):
                    share_copy(part, ring - hop if way == 0 else ring + hop, 2 * hop - 1 + way, 1 - core).wait_recv()
            share_copy(part, ring + 4, 7, 1 - core).wait_recv()

    def cross_copy(half, sec):
        first, rows = ((0, 96), (96, 160))[half]
        slot = pl.ds(pl.multiple_of((sec * POSITIONS + place) * PIECE + first, 16), rows)
        return remote(piece.at[pl.ds(first, rows)], weights.at[slot], cross_send.at[half], cross_recv.at[half], peer)

    def cross_params(sec):
        return (
            remote(gains, all_gains.at[sec], cross_send.at[2], cross_recv.at[2], peer),
            remote(biases, all_biases.at[sec], cross_send.at[3], cross_recv.at[3], peer),
        )

    def tile_rows(t):
        return pl.ds(pl.multiple_of(t * TILE, TILE), TILE)

    def raw_copy(number):
        rows = pl.ds(pl.multiple_of(number * TILE // 2, TILE // 2), TILE // 2)
        return remote(ends.at[section, rows], bufs.at[2, rows], raw_send.at[number], raw_recv.at[number], peer)

    def wait_raw(t):
        for half in range(2):
            raw_copy(2 * t + half).wait_recv()

    raw_copy(0).start()
    for r in range(64):
        reduced[32 + r : 33 + r, :] = proj_in[0:1, r * H : (r + 1) * H].astype(F32)
    for r in range(32):
        reduced[96 + r : 97 + r, :] = proj_out[0:1, 2 * r * H : (2 * r + 1) * H].astype(F32)
        reduced[128 + r : 129 + r, :] = proj_out[0:1, (2 * r + 1) * H : (2 * r + 2) * H].astype(F32)
        for slot in range(4):
            row = r if slot == 0 else 128 + 32 * slot + r
            reduced[row : row + 1, :] = conv_taps[slot : slot + 1, r * H : (r + 1) * H].astype(F32)
    piece[...] = reduced[0:PIECE, :].astype(BF16)
    for half in range(2):
        cross_copy(half, section).start()
    for copy in cross_params(section):
        copy.start()
    for number in range(1, 2 * TILES):
        raw_copy(number).start()
    own_slot = pl.ds(pl.multiple_of((section * POSITIONS + place) * PIECE, PIECE), PIECE)
    keep_piece = pltpu.make_async_copy(piece, weights.at[own_slot], local_sem.at[0])
    keep_gains = pltpu.make_async_copy(gains, all_gains.at[section], local_sem.at[1])
    keep_biases = pltpu.make_async_copy(biases, all_biases.at[section], local_sem.at[3])

    def load_own(m):
        return pltpu.make_async_copy(ends.at[m], own, local_sem.at[2])

    keep_piece.start()
    keep_gains.start()
    keep_biases.start()
    load_own(1 - section).start()
    keep_piece.wait()

    @pl.when(section == 0)
    def _():
        start_part(0)
        start_part(1)

    @pl.when(section == 1)
    def _():
        start_part(2)

    acc[...] = jnp.zeros_like(acc)
    vec[...] = jnp.zeros_like(vec)
    for half in range(2):
        cross_copy(half, 1 - section).wait_recv()

    @pl.when(section == 0)
    def _():
        start_part(2)

    @pl.when(section == 1)
    def _():
        start_part(0)
        start_part(1)

    for hop in range(1, 5):
        for part in range(3):
            advance(part, hop)
        if hop == 3:
            for part in range(3, 5):
                start_part(part)
    wait_shared(range(3))
    keep_gains.wait()
    keep_biases.wait()
    load_own(1 - section).wait()
    for copy in cross_params(1 - section):
        copy.wait_recv()

    def advance_late(hop):
        for part in range(3, 5):
            advance(part, hop)
        if hop == 4:
            wait_shared(range(3, 5))

    def matrix(sec, first, rows):
        starts = [(sec * POSITIONS + pos) * PIECE + first for pos in range(POSITIONS)]
        return jnp.concatenate([weights[start : start + rows, :] for start in starts], axis=0)

    def weight_in(block):
        return matrix(block, 32, 64)

    def weight_out(block, half):
        return matrix(block, 96 + 32 * half, 32)

    def tap(block, k):
        sec, slot = (0, k) if block == 0 and k < 4 else (1, 0) if block == 0 else (1, k + 1)
        return matrix(sec, 0 if slot == 0 else 128 + 32 * slot, 32)

    def gain(block, norm):
        first, size = ((0, D), (D, H), (D + H, H))[norm]
        return all_gains[block, :, first : first + size]

    def bias(block, norm):
        first, size = ((0, D), (2 * D, H), (2 * D + H, H))[norm]
        return all_biases[block, :, first : first + size]

    def out_bias(block, half):
        first = D + half * H
        return all_biases[block, :, first : first + H]

    def put_panels(which, base, values):
        for j in range(PANELS):
            panels[which, j, pl.ds(PAD + base, TILE), :] = values[:, j * LANES : (j + 1) * LANES]

    def get_panels(which, start):
        return jnp.concatenate([panels[which, j, pl.ds(start, TILE), :] for j in range(PANELS)], axis=1)

    def put_shift(lead, base, values):
        for j in range(PANELS):
            shift[j, pl.ds(lead + base, TILE), :] = values[:, j * LANES : (j + 1) * LANES]

    def get_shift(start):
        return jnp.concatenate([shift[j, pl.ds(start, TILE), :] for j in range(PANELS)], axis=1)

    def masked(values, base, offset):
        packed = bounds[pl.ds(base, TILE), :]
        inside = (offset >= -(packed & (LEN - 1))) & (offset <= (packed >> 10))
        return jnp.where(jnp.concatenate([inside] * PANELS, axis=1), values, 0.0).astype(BF16)

    def sentence_bounds(m):
        row = lax.broadcasted_iota(jnp.int32, (LEN, LANES), 0)
        first = jnp.zeros((LEN, LANES), jnp.int32)
        last = jnp.full((LEN, LANES), LEN, jnp.int32)
        reached = jnp.int32(0)
        for j in range(8):
            end = reached + lengths[m, j]
            inside = (row >= reached) & (row < end)
            first = jnp.where(inside, reached, first)
            last = jnp.where(inside, end, last)
            reached = end
        bounds[...] = (last - 1 - row) * LEN + row - first

    def add_product(block, first, act, grad):
        for begin in range(0, act.shape[1], CHUNK):
            rows = pl.ds(ACC_BASE[block] + first + begin, CHUNK)
            acc[rows, :] += contract_rows(act[:, begin : begin + CHUNK], grad)

    def forward_in(block, source, t, lead):
        base = pl.multiple_of(t * TILE, TILE)
        rows = pl.ds(base, TILE)
        normal, mean, scale = normalise(source[rows, :].astype(F32))
        stats[block, rows, 0:1] = mean
        stats[block, rows, 1:2] = scale
        act = gelu(normal, gain(block, 0), bias(block, 0)).astype(BF16)
        normal, _, scale = normalise(product(act, weight_in(block)))
        stats[block, rows, 2:3] = scale
        put_panels(2 * block, base, normal)
        act = gelu(normal, gain(block, 1), bias(block, 1)).astype(BF16)
        put_shift(lead, base, act.astype(F32))

    def forward_out(block, source, t, lead, store):
        base = pl.multiple_of(t * TILE, TILE)
        rows = pl.ds(base, TILE)
        conv = None
        for k in range(TAPS[block]):
            offset = (k - 2) * dilation[block]
            term = product(masked(get_shift(lead + base + offset), base, offset), tap(block, k))
            conv = term if conv is None else conv + term
        normal, _, scale = normalise(conv)
        stats[block, rows, 3:4] = scale
        put_panels(2 * block + 1, base, normal)
        if store is None:
            return
        act = gelu(normal, gain(block, 2), bias(block, 2)).astype(BF16)
        for half in range(2):
            cols = slice(half * H, (half + 1) * H)
            residual = source[rows, cols].astype(F32) + product(act, weight_out(block, half))
            store(cols, (residual + out_bias(block, half)).astype(BF16))

    def backward_out(block, grad, t, with_grads):
        base = pl.multiple_of(t * TILE, TILE)
        rows = pl.ds(base, TILE)
        upstream = contract_columns(grad[rows, 0:H], weight_out(block, 0))
        upstream = upstream + contract_columns(grad[rows, H:D], weight_out(block, 1))
        normal = get_panels(2 * block + 1, PAD + base)
        arg, rise, double_slope = gelu_parts(normal, gain(block, 2), bias(block, 2))
        double_q = upstream * double_slope
        if with_grads:
            vec[block, 0, :, D + H : 2 * D] += fold_rows(double_q * normal)
            vec[block, 1, :, D + H : 2 * D] += fold_rows(double_q)
            vec[block, 2, :, 0:D] += fold_rows(grad[rows, :].astype(F32))
            act = gelu_again(arg, rise)
            for half in range(2):
                add_product(block, D + half * H, act, grad[rows, half * H : (half + 1) * H])
        back = norm_back(normal, stats[block, rows, 3:4], gain(block, 2), double_q)
        put_panels(2 * block + 1, base, back.astype(BF16).astype(F32))

    def backward_taps(block, t, with_grads):
        base = pl.multiple_of(t * TILE, TILE)
        rows = pl.ds(base, TILE)
        normal = get_panels(2 * block, PAD + base)
        arg, rise, double_slope = gelu_parts(normal, gain(block, 1), bias(block, 1))
        if with_grads:
            act = gelu_again(arg, rise)
        upstream = None
        for k in range(TAPS[block]):
            offset = (2 - k) * dilation[block]
            moved = masked(get_panels(2 * block + 1, PAD + base + offset), base, offset)
            term = contract_columns(moved, tap(block, k))
            upstream = term if upstream is None else upstream + term
            if with_grads:
                add_product(block, 2 * D + k * H, act, moved)
        double_q = upstream * double_slope
        if with_grads:
            vec[block, 0, :, D : D + H] += fold_rows(double_q * normal)
            vec[block, 1, :, D : D + H] += fold_rows(double_q)
        middle[...] = norm_back(normal, stats[block, rows, 2:3], gain(block, 1), double_q).astype(BF16)

    def backward_in(block, source, grad, t, with_grads, store):
        base = pl.multiple_of(t * TILE, TILE)
        rows = pl.ds(base, TILE)
        back = middle[...]
        upstream = contract_columns(back, weight_in(block))
        scale = stats[block, rows, 1:2]
        normal = (source[rows, :].astype(F32) - stats[block, rows, 0:1]) * scale
        arg, rise, double_slope = gelu_parts(normal, gain(block, 0), bias(block, 0))
        double_q = upstream * double_slope
        if with_grads:
            add_product(block, 0, gelu_again(arg, rise), back)
            vec[block, 0, :, 0:D] += fold_rows(double_q * normal)
            vec[block, 1, :, 0:D] += fold_rows(double_q)
        if store is not None:
            store((grad[rows, :].astype(F32) + norm_back(normal, scale, gain(block, 0), double_q)).astype(BF16))

    def act_copy(m, t, staged):
        src = act_stage.at[lax.rem(t, 2)] if staged else bufs.at[0, tile_rows(t)]
        return pltpu.make_async_copy(src, act_out.at[m, tile_rows(t)], act_sem.at[lax.rem(t, 2)])

    def gio_copy(m, t):
        slot = lax.rem(t, 2)
        return pltpu.make_async_copy(gio_stage.at[slot], gio_out.at[m, tile_rows(t)], gio_sem.at[slot])

    def act_pass(t):
        return remote(
            act_out.at[1, tile_rows(t)], bufs.at[1, tile_rows(t)], pass_send.at[t], pass_recv.at[t], peer
        )

    def grad_pass(t):
        return remote(
            gio_out.at[0, tile_rows(t)], bufs.at[1, tile_rows(t)], pass_send.at[t], pass_recv.at[t], peer
        )

    def settle(copy, t, count):
        @pl.when(t >= 1)
        def _():
            copy(t - 1).wait()

        @pl.when(t == count - 1)
        def _():
            copy(t).wait()

    def own_piece(batch, pos):
        block, parts = BATCHES[batch]
        places = [(ACC_BASE[block] + first + size * pos, size) for first, size in parts]
        return jnp.concatenate(
            [acc[pl.ds(pl.multiple_of(first, 32), size), :] for first, size in places], axis=0
        )

    def slot_rows(batch, rows=None):
        return pl.ds(SLOT_ROW[batch], BATCH_ROWS[batch] if rows is None else rows)

    rounds = ((4,), (3, 5), (2, 6), (1, 7), (0,))

    def pair_copy(batch, number, j):
        src = red.at[2 * (number % 2) + j, slot_rows(batch)]
        dst = red.at[4 + 2 * (number % 2) + j, slot_rows(batch)]
        return remote(src, dst, pair_send.at[batch, number, j], pair_recv.at[batch, number, j], sibling)

    def send_pair(batch, number):
        for j, slot in enumerate(rounds[number]):
            if number >= 2 and j < len(rounds[number - 2]):
                pair_copy(batch, number - 2, j).wait_send()
            rows = own_piece(batch, position(ring + slot, 1 - core))
            red[2 * (number % 2) + j, slot_rows(batch), :] = rows.astype(BF16)
            pair_copy(batch, number, j).start()

    def red_copy(batch, way, step):
        rows = slot_rows(batch, BATCH_ROWS[batch] // 2 if step == 1 else None)
        src = red.at[8 + 2 * way + step % 2, rows]
        dst = red.at[12 + 2 * way + step % 2, rows]
        target = after if way == 0 else before
        return remote(src, dst, red_send.at[batch, way, step - 1], red_recv.at[batch, way, step - 1], target)

    def both_cores(batch, number, j):
        pos = position(ring + rounds[number][j], core)
        return own_piece(batch, pos) + red[4 + 2 * (number % 2) + j, slot_rows(batch), :].astype(F32)

    def arrived(batch, way, step):
        rows = BATCH_ROWS[batch]
        if step == 1:
            half = red[12 + 2 * way + 1, slot_rows(batch, rows // 2), :].astype(F32)
            blank = jnp.zeros((rows // 2, H), F32)
            return jnp.concatenate([half, blank] if way == 0 else [blank, half], axis=0)
        return red[12 + 2 * way + step % 2, slot_rows(batch), :].astype(F32)

    def begin_reduce(batch):
        if batch >= 2:
            pl.semaphore_wait(ready.at[batch - 2], 3)
        send_pair(batch, 0)

    def reduced_rows(batch, first=0, rows=None):
        return pl.ds(REDUCED_ROW[batch] + first, BATCH_ROWS[batch] if rows is None else rows)

    def reduce_step(batch, step):
        rows = BATCH_ROWS[batch]
        for j in range(len(rounds[step - 1])):
            pair_copy(batch, step - 1, j).wait_recv()
        if step > 1:
            for way in range(2):
                red_copy(batch, way, step - 1).wait_recv()
        if step == 1:
            farthest = both_cores(batch, 0, 0).astype(BF16)
            totals = [farthest[0 : rows // 2], farthest[rows // 2 : rows]]
        elif step < 5:
            totals = [
                (both_cores(batch, step - 1, way) + arrived(batch, way, step - 1)).astype(BF16) for way in range(2)
            ]
        else:
            total = both_cores(batch, 4, 0) + arrived(batch, 0, 4) + arrived(batch, 1, 4)
            reduced[reduced_rows(batch), :] = total
        if step < 5:
            for way in range(2):
                if step > 2:
                    red_copy(batch, way, step - 2).wait_send()
                red[8 + 2 * way + step % 2, slot_rows(batch, totals[way].shape[0]), :] = totals[way]
            for way in range(2):
                red_copy(batch, way, step).start()
            send_pair(batch, step)
        else:
            for way in range(2):
                for sent in (3, 4):
                    red_copy(batch, way, sent).wait_send()
            for number, j in ((2, 1), (3, 0), (3, 1), (4, 0)):
                pair_copy(batch, number, j).wait_send()
            if batch < 2:
                for target in (sibling, after, before):
                    pl.semaphore_signal(ready.at[batch], inc=1, device_id=target, device_id_type=MESH)

            @pl.when(section == 0)
            def _():
                if batch < 2:
                    send_last(batch, batch, 0, rows)
                elif batch == 3:
                    send_last(2, 3, 128, 32)

            @pl.when(section == 1)
            def _():
                if batch >= 2:
                    send_last(batch + 1, batch, 0, 128)

    def service(loop_step, when, *steps):
        @pl.when(loop_step == when)
        def _():
            for batch, step in steps:
                reduce_step(batch, step)
                if batch == 3:
                    vec_step(step)

    def vec_line(block):
        line = jnp.concatenate(
            [
                0.5 * jnp.sum(vec[block, 0], axis=0, keepdims=True),
                0.5 * jnp.sum(vec[block, 1, :, 0:D], axis=0, keepdims=True),
                jnp.sum(vec[block, 2, :, 0:D], axis=0, keepdims=True),
                0.5 * jnp.sum(vec[block, 1, :, D : 2 * D], axis=0, keepdims=True),
            ],
            axis=1,
        )
        for row in range(8):
            sums[0, 8 * block + row : 8 * block + row + 1, :] = line[:, row * 640 : (row + 1) * 640]

    def vec_share():
        return remote(sums.at[0], sums.at[1], vec_send.at[0], vec_recv.at[0], sibling)

    def vec_copy(way, hop, arriving=0):
        step = 1 if way == 0 else -1
        src = sums.at[2 + lax.rem(ring - step * (hop - 1 + arriving) + 2 * RING, RING)]
        number = 1 + 4 * way + hop - 1
        return remote(src, src, vec_send.at[number], vec_recv.at[number], after if way == 0 else before)

    def vec_step(step):
        if step == 1:
            vec_line(0)
            vec_line(1)
            vec_share().start()
            vec_share().wait_recv()
            sums[2 + ring] = sums[0] + sums[1]
        else:
            for way in range(2):
                if step < 5 or way == 0:
                    vec_copy(way, step - 1, 1).wait_recv()
        for way in range(2):
            if step < 4 or (step == 4 and way == 0):
                vec_copy(way, step).start()

    def last_copy(number):
        first, rows = ((0, 128), (128, 96), (224, 32), (0, 128), (128, 128))[number]
        part = pl.ds(first, rows)
        return remote(cross_out.at[part], cross_in.at[part], last_send.at[number], last_recv.at[number], peer)

    def send_last(number, batch, first, rows):
        begin = (0, 128, 224, 0, 128)[number]
        cross_out[begin : begin + rows, :] = reduced[reduced_rows(batch, first, rows), :].astype(BF16)
        last_copy(number).start()

    def vec_last():
        part = pl.ds(pl.multiple_of(8 - 8 * section, 8), 8)
        return remote(sums.at[0, part], sums.at[2 + RING, pl.ds(0, 8)], last_send.at[5], last_recv.at[5], peer)

    def nothing(point, t):
        pass

    def encoder_backward(m, source, grad, t, with_grads, with_store, at):
        @pl.when(t < TILES)
        def _():
            backward_out(0, grad, t, with_grads)

        at(0, t)

        @pl.when(t >= 1)
        def _():
            backward_taps(0, t - 1, with_grads)

        at(1, t)

        @pl.when(t >= 1)
        def _():
            done = t - 1

            def store(values):
                gio_stage[lax.rem(done, 2)] = values

            backward_in(0, source, grad, done, with_grads, store if with_store else None)
            if with_store:
                gio_copy(m, done).start()
                settle(lambda s: gio_copy(m, s), done, TILES)

        at(2, t)

    def decoder_services(point, t):
        if point == 0:
            service(t, 0, (0, 1), (1, 1))
        else:
            for step in range(2, 6):
                service(t, step - 1, (point - 1, step))

    @pl.when(section == 0)
    def _():
        sentence_bounds(1)

        def encoder_forward(m, t, at):
            @pl.when(t < TILES)
            def _():
                forward_in(0, own, t, LEAD)

            at(0, t)

            @pl.when(t >= 1)
            def _():
                done = t - 1

                def store(cols, values):
                    bufs[0, tile_rows(done), cols] = values

                forward_out(0, own, done, LEAD, store)
                act_copy(m, done, False).start()
                settle(lambda s: act_copy(m, s, False), done, TILES)

            at(1, t)

        @pl.loop(0, TILES + 1)
        def _(t):
            encoder_forward(1, t, nothing)
            for hop in range(1, 5):

                @pl.when(t == hop)
                def _():
                    advance_late(hop)

        for t in range(TILES):
            act_pass(t).start()

        @pl.loop(0, TILES + 1)
        def _(t):
            @pl.when(t < TILES)
            def _():
                wait_raw(t)
                forward_in(1, bufs.at[0], t, LEAD)
                forward_out(1, bufs.at[0], t, LEAD, None)
                backward_out(1, bufs.at[2], t, True)

            @pl.when(t >= 1)
            def _():
                done = t - 1

                def store(values):
                    bufs[2, tile_rows(done), :] = values

                backward_taps(1, done, True)
                backward_in(1, bufs.at[0], bufs.at[2], done, True, store)

        begin_reduce(0)
        begin_reduce(1)

        @pl.loop(0, TILES + 1)
        def _(t):
            encoder_backward(1, own, bufs.at[2], t, True, True, decoder_services)

        load_own(0).start()
        begin_reduce(2)
        begin_reduce(3)
        sentence_bounds(0)
        load_own(0).wait()

        def forward_services(point, t):
            if point == 0:
                service(t, 0, (2, 1), (3, 1))
                service(t, 3, (2, 3))
            else:
                service(t, 1, (2, 2))
                service(t, 2, (3, 2))
                service(t, 3, (3, 3))
                service(t, 4, (2, 4))

        @pl.loop(0, TILES + 1)
        def _(t):
            encoder_forward(0, t, forward_services)

        def backward_services(point, t):
            if point == 0:
                service(t, 0, (3, 4))
            else:
                service(t, 1, (point + 1, 5))

        @pl.loop(0, TILES + 1)
        def _(t):
            @pl.when(t < TILES)
            def _():
                grad_pass(t).wait_recv()

            encoder_backward(0, own, bufs.at[1], t, False, True, backward_services)

        for t in range(TILES):
            act_pass(t).wait_send()

    @pl.when(section == 1)
    def _():
        sentence_bounds(0)

        def decoder_forward(m, source, t, lead, at):
            def store(cols, values):
                act_stage[lax.rem(t, 2), :, cols] = values

            forward_in(1, source, t, lead)
            at(0, t)
            forward_out(1, source, t, lead, store)
            act_copy(m, t, True).start()
            settle(lambda s: act_copy(m, s, True), t, TILES)

        @pl.loop(0, TILES + 2)
        def _(t):
            @pl.when(t < TILES)
            def _():
                wait_raw(t)
                forward_in(0, bufs.at[2], t, LEAD)

            @pl.when((t >= 1) & (t <= TILES))
            def _():
                done = t - 1

                def store(cols, values):
                    bufs[0, tile_rows(done), cols] = values

                forward_out(0, bufs.at[2], done, LEAD, store)

            @pl.when(t == 0)
            def _():
                advance_late(1)

            @pl.when(t == 1)
            def _():
                for hop in range(2, 5):
                    advance_late(hop)

            @pl.when((t >= 1) & (t <= TILES))
            def _():
                decoder_forward(0, bufs.at[0], t - 1, LEAD - TILE, nothing)
                backward_out(1, own, t - 1, True)

            @pl.when(t >= 2)
            def _():
                done = t - 2

                def store(values):
                    gio_stage[lax.rem(done, 2)] = values
                    own[tile_rows(done), :] = values

                backward_taps(1, done, True)
                backward_in(1, bufs.at[0], own, done, True, store)
                gio_copy(0, done).start()
                settle(lambda s: gio_copy(0, s), done, TILES)

                @pl.when(done >= 1)
                def _():
                    grad_pass(done - 1).start()

        grad_pass(TILES - 1).start()
        begin_reduce(0)
        begin_reduce(1)

        @pl.loop(0, TILES + 1)
        def _(t):
            encoder_backward(0, bufs.at[2], own, t, True, False, decoder_services)

        load_own(1).start()
        begin_reduce(2)
        begin_reduce(3)
        sentence_bounds(1)
        load_own(1).wait()

        def encoder_services(point, t):
            if point == 0:
                service(t, 0, (2, 1), (3, 1))
                for when in range(1, 4):
                    service(t, when, (3, when + 1))
            elif point == 1:
                for when in range(0, 4):
                    service(t, when, (2, when + 2))
            else:
                service(t, 3, (3, 5))

        @pl.loop(0, TILES + 1)
        def _(t):
            @pl.when(t < TILES)
            def _():
                act_pass(t).wait_recv()
                decoder_forward(1, bufs.at[1], t, LEAD, encoder_services)
                backward_out(1, own, t, False)

            encoder_services(1, t)

            @pl.when(t >= 1)
            def _():
                done = t - 1

                def store(values):
                    gio_stage[lax.rem(done, 2)] = values

                backward_taps(1, done, False)
                backward_in(1, bufs.at[1], own, done, False, store)
                gio_copy(1, done).start()
                settle(lambda s: gio_copy(1, s), done, TILES)

            encoder_services(2, t)

        for t in range(TILES):
            grad_pass(t).wait_send()

    vec_share().wait_send()
    total = sums[2]
    for chip_sum in range(1, RING):
        total = total + sums[2 + chip_sum]
    sums[0] = total
    vec_last().start()

    @pl.when(section == 0)
    def _():
        last_copy(3).wait_recv()
        last_copy(4).wait_recv()
        terms = [reduced[reduced_rows(2), :], reduced[reduced_rows(3, 0, 128), :]]
        total = jnp.concatenate(terms, axis=0) + cross_in[...].astype(F32)
        grads_out[...] = jnp.concatenate([total[128:192], total[0:128], total[192:256]], axis=0)

    @pl.when(section == 1)
    def _():
        for number in range(3):
            last_copy(number).wait_recv()
        terms = [reduced[reduced_rows(0), :], reduced[reduced_rows(1), :], reduced[reduced_rows(3, 128, 32), :]]
        grads_out[...] = jnp.concatenate(terms, axis=0) + cross_in[...].astype(F32)

    vec_last().wait_recv()
    line = sums[0, pl.ds(pl.multiple_of(8 * section, 8), 8), :] + sums[2 + RING, 0:8, :]
    line_out[...] = line

    for part in range(5):
        for hop in range(1, 5):
            for way in range(2):
                ring_copy(part, hop, way).wait_send()
        share_copy(part, ring, 0, core).wait_send()
        for slot in range(1, 8):
            share_copy(part, ring, slot, core).wait_send()
    for half in range(2):
        cross_copy(half, section).wait_send()
    for copy in cross_params(section):
        copy.wait_send()
    for number in range(2 * TILES):
        raw_copy(number).wait_send()
    for way in range(2):
        for hop in range(1, 5 if way == 0 else 4):
            vec_copy(way, hop).wait_send()
    vec_last().wait_send()

    @pl.when(section == 0)
    def _():
        for number in range(3):
            last_copy(number).wait_send()

    @pl.when(section == 1)
    def _():
        for number in range(3, 5):
            last_copy(number).wait_send()


def finish_kernel(act, gio, grads, line, act_out, gio_out, in_out, out_out, tap_out, gain_out, bias_out):
    act_out[...] = act[...]
    gio_out[...] = gio[...].astype(F32)

    for step in range(8):

        @pl.when(pl.program_id(0) == step)
        def _():
            for r in range(8 * step, 8 * step + 8):
                in_out[:, r * H : (r + 1) * H] = grads[r : r + 1, :]
            for r in range(4 * step, 4 * step + 4):
                for half in range(2):
                    row = 64 + 32 * half + r
                    out_out[:, (2 * r + half) * H : (2 * r + half + 1) * H] = grads[row : row + 1, :]
                for number, slot in enumerate((1, 2, 3, 0)):
                    row = 128 + 32 * number + r
                    tap_out[slot : slot + 1, r * H : (r + 1) * H] = grads[row : row + 1, :]
            if step == 0:
                flat = jnp.concatenate([line[row : row + 1, :] for row in range(8)], axis=1)
                gain_out[...] = flat[:, 0 : 2 * D]
                bias_out[...] = flat[:, 2 * D : 5 * D]


def finish(act, gio, grads, line):
    micro, rows = act.shape[:2]
    shape = jax.ShapeDtypeStruct
    tiles = pl.BlockSpec((micro * rows // 8, D), lambda t: (t, 0))
    whole = pl.BlockSpec(memory_space=pltpu.VMEM)
    flat = (micro * rows, D)
    act, gio, *rest = pl.pallas_call(
        finish_kernel,
        grid=(8,),
        out_shape=[
            shape(flat, BF16),
            shape(flat, F32),
            shape((1, 64 * H), F32),
            shape((1, 64 * H), F32),
            shape((4, 32 * H), F32),
            shape((1, 2 * D), F32),
            shape((1, 3 * D), F32),
        ],
        in_specs=[tiles, tiles, whole, whole],
        out_specs=[tiles, tiles] + [whole] * 5,
        compiler_params=pltpu.CompilerParams(vmem_limit_bytes=64 << 20),
        name="finish",
    )(act.reshape(flat), gio.reshape(flat), grads, line)
    return (act.reshape(micro, rows, D), gio.reshape(micro, rows, D), *rest)


def local(group, block_ends, proj_in, proj_out, conv_taps, norm_gains, bias_terms, lengths, dilation):
    micro, rows = block_ends.shape[1:3]
    if group > 1:
        proj_in = lax.all_gather(proj_in, "lane", axis=1, tiled=True)
        proj_out = lax.all_gather(proj_out, "lane", axis=1, tiled=True)
        conv_taps = lax.all_gather(conv_taps, "lane", axis=2, tiled=True)
    vmem = pl.BlockSpec(memory_space=pltpu.VMEM)
    smem = pl.BlockSpec(memory_space=pltpu.SMEM)
    hbm = pl.BlockSpec(memory_space=pl.ANY)
    shape = jax.ShapeDtypeStruct
    dma = pltpu.SemaphoreType.DMA
    act, gio, grads, line = pl.pallas_call(
        functools.partial(kernel, group),
        out_shape=[
            shape((micro, rows, D), BF16),
            shape((micro, rows, D), BF16),
            shape((256, H), F32),
            shape((8, 640), F32),
        ],
        in_specs=[smem, smem, hbm, vmem, vmem, vmem, vmem, vmem],
        out_specs=[hbm, hbm, vmem, vmem],
        scratch_shapes=[
            pltpu.VMEM((2 * POSITIONS * PIECE, H), BF16),
            pltpu.VMEM((LEN, D), BF16),
            pltpu.VMEM((3, LEN, D), BF16),
            pltpu.VMEM((4, PANELS, LEN + 2 * PAD, LANES), F32),
            pltpu.VMEM((PANELS, LEAD + LEN + PAD, LANES), F32),
            pltpu.VMEM((2, LEN, LANES), F32),
            pltpu.VMEM((LEN, LANES), jnp.int32),
            pltpu.VMEM((ACC_ROWS, H), F32),
            pltpu.VMEM((2, 3, 8, 2 * D), F32),
            pltpu.VMEM((2, TILE, D), BF16),
            pltpu.VMEM((2, TILE, D), BF16),
            pltpu.VMEM((2, 1, 2 * D), F32),
            pltpu.VMEM((2, 1, 3 * D), F32),
            pltpu.VMEM((3 + RING, 16, 640), F32),
            pltpu.VMEM((16, MOST, H), BF16),
            pltpu.VMEM((REDUCED, H), F32),
            pltpu.VMEM((256, H), BF16),
            pltpu.VMEM((256, H), BF16),
            pltpu.VMEM((PIECE, H), BF16),
            pltpu.VMEM((TILE, H), BF16),
            dma((2, 5, 4)),
            dma((2, 5, 4)),
            dma((5, 8)),
            dma((5, 8)),
            dma((4,)),
            dma((4,)),
            dma((2 * TILES,)),
            dma((2 * TILES,)),
            dma((TILES,)),
            dma((TILES,)),
            dma((4,)),
            dma((2,)),
            dma((2,)),
            dma((4, 2, 4)),
            dma((4, 2, 4)),
            dma((4, 5, 2)),
            dma((4, 5, 2)),
            dma((9,)),
            dma((9,)),
            dma((6,)),
            dma((6,)),
            pltpu.SemaphoreType.REGULAR((2,)),
        ],
        compiler_params=pltpu.CompilerParams(
            collective_id=0, has_side_effects=True, vmem_limit_bytes=64 << 20
        ),
        name="residual_blocks",
    )(dilation, lengths[:, 0, :], block_ends[0], proj_in, proj_out, conv_taps[0], norm_gains, bias_terms)
    act, gio, *grads, gain_sum, bias_sum = finish(act, gio, grads, line)
    grads[2] = grads[2][None]
    if group > 1:
        grads = tuple(
            lax.psum_scatter(part, "lane", scatter_dimension=part.ndim - 1, tiled=True) for part in grads
        )
        gain_sum, bias_sum = lax.psum((gain_sum, bias_sum), "lane")
    return (act[None], gio[None], *grads, gain_sum, bias_sum)


def solution(mesh):
    group = mesh.shape["dp"] // POSITIONS
    spread = "dp"
    if group > 1:
        mesh = Mesh(mesh.devices.reshape(2, POSITIONS, group), ("section", "dp", "lane"))
        spread = ("dp", "lane")
    placed = (
        P("section", None, spread, None),
        P("section", spread),
        P("section", spread),
        P("section", None, spread),
        P("section", None),
        P("section", None),
        P(None, spread, None),
        P(),
    )
    return jax.shard_map(
        functools.partial(local, group),
        mesh=mesh,
        in_specs=placed,
        out_specs=(
            P("section", None, spread, None),
            P("section", None, spread, None),
            P("section", spread),
            P("section", spread),
            P("section", None, spread),
            P("section", None),
            P("section", None),
        ),
        check_vma=False,
    )
```

```python
import functools

import jax
import jax.numpy as jnp
from jax import lax
from jax.experimental import pallas as pl
from jax.experimental.pallas import tpu as pltpu
from jax.sharding import Mesh
from jax.sharding import PartitionSpec as P

D = 1024
H = 512
LEN = 1024
POSITIONS = 16
RING = 8
TILE = 256
TILES = LEN // TILE
PAD = 128
CHUNK = 256
LANES = 128
PANELS = H // LANES
epsilon = 1e-05
linear_term = 0.7978845608028654
cubic_term = linear_term * 0.044715
kappa = cubic_term ** (1.0 / 3.0)
beta = linear_term / kappa
MESH = pl.DeviceIdType.MESH
F32 = jnp.float32
BF16 = jnp.bfloat16

PIECE = 256
EARLY = ((0, 0, 96), (0, 96, 160), (1, 0, 32))
LATE = ((1, 32, 64), (1, 96, 160))
PARTS = EARLY + LATE
TAPS = (5, 3)
ACC_BASE = (0, 2 * D + 5 * H)
ACC_ROWS = 4 * D + 8 * H
BATCHES = (
    (1, ((0, 64), (D, 32), (D + H, 32))),
    (1, ((2 * D, 32), (2 * D + H, 32), (2 * D + 2 * H, 32))),
    (0, ((D, 32), (D + H, 32), (2 * D + H, 32), (2 * D + 2 * H, 32))),
    (0, ((0, 64), (2 * D + 3 * H, 32), (2 * D, 32), (2 * D + 4 * H, 32))),
)
BATCH_ROWS = (128, 96, 128, 160)
SLOT_ROW = (0, 128, 0, 128)
REDUCED_ROW = (0, 128, 224, 352)
REDUCED = 512
MOST = 288
LEAD = 384


def aligned(start, size):
    return start if isinstance(start, int) else pl.multiple_of(start, size)


def steps(count, unroll):
    def run(body):
        if not unroll:
            return pl.loop(0, count)(body)
        for t in range(count):
            body(t)

    return run


def product(left, right):
    return jnp.dot(left, right, preferred_element_type=F32)


def contract_rows(left, right):
    return lax.dot_general(left, right, (((0,), (0,)), ((), ())), preferred_element_type=F32)


def contract_columns(left, right):
    return lax.dot_general(left, right, (((1,), (1,)), ((), ())), preferred_element_type=F32)


def normalise(values):
    mean = jnp.mean(values, axis=-1, keepdims=True)
    centre = values - mean
    scale = lax.rsqrt(jnp.mean(centre * centre, axis=-1, keepdims=True) + epsilon)
    return centre * scale, mean, scale


def gelu(normal, gain, bias):
    half = normal * (0.5 * gain) + 0.5 * bias
    inner = half * (half * half * (8.0 * cubic_term) + 2.0 * linear_term)
    return half + half * jnp.tanh(inner)


def gelu_parts(normal, gain, bias):
    arg = normal * (kappa * gain) + kappa * bias
    square = arg * arg
    rise = 1.0 + jnp.tanh(arg * (square + beta))
    double_slope = rise * (1.0 + (2.0 - rise) * (arg * (3.0 * square + beta)))
    return arg, rise, double_slope


def gelu_again(arg, rise):
    return (arg * rise * (0.5 / kappa)).astype(BF16)


def norm_back(normal, scale, gain, double_q):
    weighted = (0.5 * gain) * double_q
    count = 1.0 / normal.shape[-1]
    mean = jnp.sum(weighted, axis=-1, keepdims=True) * count
    along = jnp.sum(weighted * normal, axis=-1, keepdims=True) * count
    return (weighted - mean - normal * along) * scale


def fold_rows(values):
    return jnp.sum(values.reshape(values.shape[0] // 8, 8, values.shape[1]), axis=0)


def ring_chip(place):
    place = lax.rem(place + 2 * RING, RING)
    return jnp.where(place < RING // 2, 2 * place, 2 * (RING - place) - 1)


def kernel(group, dilation, lengths, ends, proj_in, proj_out, conv_taps, gains, biases, *refs):
    (
        act_out,
        gio_out,
        grads_out,
        line_out,
        parked,
        weights,
        own,
        bufs,
        panel_0,
        panel_1,
        panel_2,
        panel_3,
        shift,
        stats,
        bounds,
        acc,
        vec,
        gio_stage,
        act_stage,
        all_gains,
        all_biases,
        sums,
        red,
        reduced,
        cross_out,
        cross_in,
        piece,
        middle,
        ring_send,
        ring_recv,
        sib_send,
        sib_recv,
        cross_send,
        cross_recv,
        raw_send,
        raw_recv,
        pass_send,
        pass_recv,
        local_sem,
        spare_sem,
        park_sem,
        act_sem,
        gio_sem,
        red_send,
        red_recv,
        pair_send,
        pair_recv,
        vec_send,
        vec_recv,
        last_send,
        last_recv,
        ready,
    ) = refs
    panels = (panel_0, panel_1, panel_2, panel_3)
    section = lax.axis_index("section")
    index = lax.axis_index("dp")
    place, lane = index // group, lax.rem(index, group)
    chip, core = place // 2, lax.rem(place, 2)
    ring = jnp.where(lax.rem(chip, 2) == 0, chip // 2, RING - (chip + 1) // 2)

    def device(sec, position):
        return {"section": sec, "dp": position * group + lane}

    def position(ring_place, which_core):
        return 2 * ring_chip(ring_place) + which_core

    peer = device(1 - section, place)
    sibling = device(section, 2 * chip + 1 - core)
    after = device(section, position(ring + 1, core))
    before = device(section, position(ring - 1, core))

    def remote(src, dst, send, recv, target):
        return pltpu.make_async_remote_copy(
            src_ref=src, dst_ref=dst, send_sem=send, recv_sem=recv, device_id=target, device_id_type=MESH
        )

    barrier = pltpu.get_barrier_semaphore()
    for target in (peer, sibling, after, before):
        pl.semaphore_signal(barrier, inc=1, device_id=target, device_id_type=MESH)
    def lay_out(row, values):
        reduced[row : row + 1, :] = values.astype(F32)

    for r in range(32):
        lay_out(r, conv_taps[0:1, r * H : (r + 1) * H])
    for r in range(64):
        lay_out(32 + r, proj_in[0:1, r * H : (r + 1) * H])
    piece[0:96, :] = reduced[0:96, :].astype(BF16)
    pl.semaphore_wait(barrier, 4)

    def rows_of(part, origin, half=None):
        sec, first, rows = PARTS[part]
        if half is not None:
            first, rows = first + half * (rows // 2), rows // 2
        return pl.ds(pl.multiple_of((sec * POSITIONS + origin) * PIECE + first, 16), rows)

    def ring_copy(part, hop, way):
        step = 1 if way == 0 else -1
        rows = rows_of(part, position(ring - step * (hop - 1), core), way if hop == 4 else None)
        return remote(
            weights.at[rows], weights.at[rows], ring_send.at[way, part, hop - 1], ring_recv.at[way, part, hop - 1],
            after if way == 0 else before,
        )

    def ring_arrival(part, hop, way):
        step = 1 if way == 0 else -1
        rows = rows_of(part, position(ring - step * hop, core), way if hop == 4 else None)
        return remote(
            weights.at[rows], weights.at[rows], ring_send.at[way, part, hop - 1], ring_recv.at[way, part, hop - 1],
            after if way == 0 else before,
        )

    def share_copy(part, ring_place, slot, which_core):
        rows = rows_of(part, position(ring_place, which_core))
        return remote(
            weights.at[rows], weights.at[rows], sib_send.at[part, slot], sib_recv.at[part, slot], sibling
        )

    def start_part(part):
        for way in range(2):
            ring_copy(part, 1, way).start()
        share_copy(part, ring, 0, core).start()

    def advance(part, hop):
        for way in range(2):
            ring_arrival(part, hop, way).wait_recv()
            if hop < 4:
                ring_copy(part, hop + 1, way).start()
                share_copy(part, ring - hop if way == 0 else ring + hop, 2 * hop - 1 + way, core).start()
        if hop == 4:
            share_copy(part, ring + 4, 7, core).start()

    def wait_shared(parts):
        for part in parts:
            share_copy(part, ring, 0, 1 - core).wait_recv()
            for hop in range(1, 4):
                for way in range(2):
                    share_copy(part, ring - hop if way == 0 else ring + hop, 2 * hop - 1 + way, 1 - core).wait_recv()
            share_copy(part, ring + 4, 7, 1 - core).wait_recv()

    def cross_copy(half, sec):
        first, rows = ((0, 96), (96, 160))[half]
        slot = pl.ds(pl.multiple_of((sec * POSITIONS + place) * PIECE + first, 16), rows)
        return remote(piece.at[pl.ds(first, rows)], weights.at[slot], cross_send.at[half], cross_recv.at[half], peer)

    def cross_params(sec):
        return (
            remote(gains, all_gains.at[sec], cross_send.at[2], cross_recv.at[2], peer),
            remote(biases, all_biases.at[sec], cross_send.at[3], cross_recv.at[3], peer),
        )

    def tile_rows(t):
        return pl.ds(aligned(t * TILE, TILE), TILE)

    def raw_copy(number):
        rows = pl.ds(aligned(number * (TILE // 2), TILE // 2), TILE // 2)
        return remote(ends.at[section, rows], bufs.at[2, rows], raw_send.at[number], raw_recv.at[number], peer)

    def wait_raw(t):
        for half in range(2):
            raw_copy(2 * t + half).wait_recv()

    def own_slot(half):
        first, rows = ((0, 96), (96, 160))[half]
        slot = pl.ds(pl.multiple_of((section * POSITIONS + place) * PIECE + first, 16), rows)
        return pltpu.make_async_copy(piece.at[pl.ds(first, rows)], weights.at[slot], local_sem.at[0 if half == 0 else 4])

    keep_gains = pltpu.make_async_copy(gains, all_gains.at[section], local_sem.at[1])
    keep_biases = pltpu.make_async_copy(biases, all_biases.at[section], local_sem.at[3])

    def load_own(m):
        return pltpu.make_async_copy(ends.at[m], own, local_sem.at[2])

    cross_copy(0, section).start()
    own_slot(0).start()
    own_slot(0).wait()

    @pl.when(section == 0)
    def _():
        start_part(0)

    @pl.when(section == 1)
    def _():
        start_part(2)

    for r in range(32):
        for half in range(2):
            first = (2 * r + half) * H
            lay_out(96 + 32 * half + r, proj_out[0:1, first : first + H])
        for slot in range(1, 4):
            lay_out(128 + 32 * slot + r, conv_taps[slot : slot + 1, r * H : (r + 1) * H])
    piece[96:PIECE, :] = reduced[96:PIECE, :].astype(BF16)
    cross_copy(1, section).start()
    own_slot(1).start()
    for copy in cross_params(section):
        copy.start()
    for number in range(2 * TILES):
        raw_copy(number).start()
    keep_gains.start()
    keep_biases.start()
    load_own(1 - section).start()
    own_slot(1).wait()

    @pl.when(section == 0)
    def _():
        start_part(1)

    acc[...] = jnp.zeros_like(acc)
    vec[...] = jnp.zeros_like(vec)
    cross_copy(0, 1 - section).wait_recv()

    @pl.when(section == 0)
    def _():
        start_part(2)

    @pl.when(section == 1)
    def _():
        start_part(0)

    cross_copy(1, 1 - section).wait_recv()

    @pl.when(section == 1)
    def _():
        start_part(1)

    for hop in range(1, 4):
        for part in range(3):
            advance(part, hop)
    start_part(3)
    advance(0, 4)
    start_part(4)
    wait_shared([0])
    keep_gains.wait()
    keep_biases.wait()
    load_own(1 - section).wait()
    for copy in cross_params(1 - section):
        copy.wait_recv()

    def finish_early():
        for part in range(1, 3):
            advance(part, 4)
        wait_shared(range(1, 3))

    def advance_late(hop):
        for part in range(3, 5):
            advance(part, hop)
        if hop == 4:
            wait_shared(range(3, 5))

    def matrix(sec, first, rows):
        starts = [(sec * POSITIONS + pos) * PIECE + first for pos in range(POSITIONS)]
        return jnp.concatenate([weights[start : start + rows, :] for start in starts], axis=0)

    def weight_in(block):
        return matrix(block, 32, 64)

    def weight_out(block, half):
        return matrix(block, 96 + 32 * half, 32)

    def tap(block, k):
        sec, slot = (0, k) if block == 0 and k < 4 else (1, 0) if block == 0 else (1, k + 1)
        return matrix(sec, 0 if slot == 0 else 128 + 32 * slot, 32)

    def gain(block, norm):
        first, size = ((0, D), (D, H), (D + H, H))[norm]
        return all_gains[block, :, first : first + size]

    def bias(block, norm):
        first, size = ((0, D), (2 * D, H), (2 * D + H, H))[norm]
        return all_biases[block, :, first : first + size]

    def out_bias(block, half):
        first = D + half * H
        return all_biases[block, :, first : first + H]

    def put_panels(which, base, values):
        for j in range(PANELS):
            panels[which][j, pl.ds(PAD + base, TILE), :] = values[:, j * LANES : (j + 1) * LANES]

    def get_panels(which, start):
        return jnp.concatenate([panels[which][j, pl.ds(start, TILE), :] for j in range(PANELS)], axis=1)

    def put_shift(lead, base, values):
        for j in range(PANELS):
            shift[j, pl.ds(lead + base, TILE), :] = values[:, j * LANES : (j + 1) * LANES]

    def get_shift(start):
        return jnp.concatenate([shift[j, pl.ds(start, TILE), :] for j in range(PANELS)], axis=1)

    def masked(m, values, base, offset):
        packed = bounds[m, pl.ds(base, TILE), :]
        inside = (offset >= -(packed & (LEN - 1))) & (offset <= (packed >> 10))
        return jnp.where(jnp.concatenate([inside] * PANELS, axis=1), values, 0.0).astype(BF16)

    def sentence_bounds(m):
        row = lax.broadcasted_iota(jnp.int32, (LEN, LANES), 0)
        first = jnp.zeros((LEN, LANES), jnp.int32)
        last = jnp.full((LEN, LANES), LEN, jnp.int32)
        reached = jnp.int32(0)
        for j in range(8):
            end = reached + lengths[m, j]
            inside = (row >= reached) & (row < end)
            first = jnp.where(inside, reached, first)
            last = jnp.where(inside, end, last)
            reached = end
        bounds[m] = (last - 1 - row) * LEN + row - first

    def add_product(block, first, act, grad):
        for begin in range(0, act.shape[1], CHUNK):
            rows = pl.ds(ACC_BASE[block] + first + begin, CHUNK)
            acc[rows, :] += contract_rows(act[:, begin : begin + CHUNK], grad)

    def forward_in(run, read, t, lead):
        block, _, pair, stat = run
        base = aligned(t * TILE, TILE)
        rows = pl.ds(base, TILE)
        normal, mean, scale = normalise(read(t, slice(0, D)).astype(F32))
        stats[stat, rows, 0:1] = mean
        stats[stat, rows, 1:2] = scale
        act = gelu(normal, gain(block, 0), bias(block, 0)).astype(BF16)
        normal, _, scale = normalise(product(act, weight_in(block)))
        stats[stat, rows, 2:3] = scale
        put_panels(2 * pair, base, normal)
        act = gelu(normal, gain(block, 1), bias(block, 1)).astype(BF16)
        put_shift(lead, base, act.astype(F32))

    def forward_out(run, read, t, lead, store):
        block, m, pair, stat = run
        base = aligned(t * TILE, TILE)
        rows = pl.ds(base, TILE)
        conv = None
        for k in range(TAPS[block]):
            offset = (k - 2) * dilation[block]
            term = product(masked(m, get_shift(lead + base + offset), base, offset), tap(block, k))
            conv = term if conv is None else conv + term
        normal, _, scale = normalise(conv)
        stats[stat, rows, 3:4] = scale
        put_panels(2 * pair + 1, base, normal)
        if store is None:
            return
        act = gelu(normal, gain(block, 2), bias(block, 2)).astype(BF16)
        for half in range(2):
            cols = slice(half * H, (half + 1) * H)
            residual = read(t, cols).astype(F32) + product(act, weight_out(block, half))
            store(cols, (residual + out_bias(block, half)).astype(BF16))

    def backward_out(run, grad, t, with_grads):
        block, _, pair, stat = run
        base = aligned(t * TILE, TILE)
        rows = pl.ds(base, TILE)
        upstream = contract_columns(grad[rows, 0:H], weight_out(block, 0))
        upstream = upstream + contract_columns(grad[rows, H:D], weight_out(block, 1))
        normal = get_panels(2 * pair + 1, PAD + base)
        arg, rise, double_slope = gelu_parts(normal, gain(block, 2), bias(block, 2))
        double_q = upstream * double_slope
        if with_grads:
            vec[block, 0, :, D + H : 2 * D] += fold_rows(double_q * normal)
            vec[block, 1, :, D + H : 2 * D] += fold_rows(double_q)
            vec[block, 2, :, 0:D] += fold_rows(grad[rows, :].astype(F32))
            act = gelu_again(arg, rise)
            for half in range(2):
                add_product(block, D + half * H, act, grad[rows, half * H : (half + 1) * H])
        back = norm_back(normal, stats[stat, rows, 3:4], gain(block, 2), double_q)
        put_panels(2 * pair + 1, base, back.astype(BF16).astype(F32))

    def backward_taps(run, t, with_grads):
        block, m, pair, stat = run
        base = aligned(t * TILE, TILE)
        rows = pl.ds(base, TILE)
        normal = get_panels(2 * pair, PAD + base)
        arg, rise, double_slope = gelu_parts(normal, gain(block, 1), bias(block, 1))
        if with_grads:
            act = gelu_again(arg, rise)
        upstream = None
        for k in range(TAPS[block]):
            offset = (2 - k) * dilation[block]
            moved = masked(m, get_panels(2 * pair + 1, PAD + base + offset), base, offset)
            term = contract_columns(moved, tap(block, k))
            upstream = term if upstream is None else upstream + term
            if with_grads:
                add_product(block, 2 * D + k * H, act, moved)
        double_q = upstream * double_slope
        if with_grads:
            vec[block, 0, :, D : D + H] += fold_rows(double_q * normal)
            vec[block, 1, :, D : D + H] += fold_rows(double_q)
        middle[...] = norm_back(normal, stats[stat, rows, 2:3], gain(block, 1), double_q).astype(BF16)

    def backward_in(run, source, grad, t, with_grads, store):
        block, _, _, stat = run
        base = aligned(t * TILE, TILE)
        rows = pl.ds(base, TILE)
        back = middle[...]
        upstream = contract_columns(back, weight_in(block))
        scale = stats[stat, rows, 1:2]
        normal = (source[rows, :].astype(F32) - stats[stat, rows, 0:1]) * scale
        arg, rise, double_slope = gelu_parts(normal, gain(block, 0), bias(block, 0))
        double_q = upstream * double_slope
        if with_grads:
            add_product(block, 0, gelu_again(arg, rise), back)
            vec[block, 0, :, 0:D] += fold_rows(double_q * normal)
            vec[block, 1, :, 0:D] += fold_rows(double_q)
        if store is not None:
            store((grad[rows, :].astype(F32) + norm_back(normal, scale, gain(block, 0), double_q)).astype(BF16))

    def reader(ref):
        return lambda t, cols: ref[tile_rows(t), cols]

    def act_copy(m, t, staged):
        src = act_stage.at[t % 2] if staged else bufs.at[0, tile_rows(t)]
        return pltpu.make_async_copy(src, act_out.at[m, tile_rows(t)], act_sem.at[t % 2])

    def gio_copy(m, t):
        slot = t % 2
        return pltpu.make_async_copy(gio_stage.at[slot], gio_out.at[m, tile_rows(t)], gio_sem.at[slot])

    def act_pass(t):
        return remote(
            act_out.at[1, tile_rows(t)], bufs.at[1, tile_rows(t)], pass_send.at[t], pass_recv.at[t], peer
        )

    def grad_pass(t):
        return remote(
            gio_out.at[0, tile_rows(t)], bufs.at[1, tile_rows(t)], pass_send.at[t], pass_recv.at[t], peer
        )

    def settle(copy, t, count):
        @pl.when(t >= 1)
        def _():
            copy(t - 1).wait()

        @pl.when(t == count - 1)
        def _():
            copy(t).wait()

    def own_piece(batch, pos):
        block, parts = BATCHES[batch]
        places = [(ACC_BASE[block] + first + size * pos, size) for first, size in parts]
        return jnp.concatenate(
            [acc[pl.ds(pl.multiple_of(first, 32), size), :] for first, size in places], axis=0
        )

    def slot_rows(batch, rows=None):
        return pl.ds(SLOT_ROW[batch], BATCH_ROWS[batch] if rows is None else rows)

    rounds = ((4,), (3, 5), (2, 6), (1, 7), (0,))

    def pair_copy(batch, number, j):
        src = red.at[2 * (number % 2) + j, slot_rows(batch)]
        dst = red.at[4 + 2 * (number % 2) + j, slot_rows(batch)]
        return remote(src, dst, pair_send.at[batch, number, j], pair_recv.at[batch, number, j], sibling)

    def send_pair(batch, number):
        for j, slot in enumerate(rounds[number]):
            if number >= 2 and j < len(rounds[number - 2]):
                pair_copy(batch, number - 2, j).wait_send()
            rows = own_piece(batch, position(ring + slot, 1 - core))
            red[2 * (number % 2) + j, slot_rows(batch), :] = rows.astype(BF16)
            pair_copy(batch, number, j).start()

    def red_copy(batch, way, step):
        rows = slot_rows(batch, BATCH_ROWS[batch] // 2 if step == 1 else None)
        src = red.at[8 + 2 * way + step % 2, rows]
        dst = red.at[12 + 2 * way + step % 2, rows]
        target = after if way == 0 else before
        return remote(src, dst, red_send.at[batch, way, step - 1], red_recv.at[batch, way, step - 1], target)

    def both_cores(batch, number, j):
        pos = position(ring + rounds[number][j], core)
        return own_piece(batch, pos) + red[4 + 2 * (number % 2) + j, slot_rows(batch), :].astype(F32)

    def arrived(batch, way, step):
        rows = BATCH_ROWS[batch]
        if step == 1:
            half = red[12 + 2 * way + 1, slot_rows(batch, rows // 2), :].astype(F32)
            blank = jnp.zeros((rows // 2, H), F32)
            return jnp.concatenate([half, blank] if way == 0 else [blank, half], axis=0)
        return red[12 + 2 * way + step % 2, slot_rows(batch), :].astype(F32)

    def begin_reduce(batch):
        if batch >= 2:
            pl.semaphore_wait(ready.at[batch - 2], 3)
        send_pair(batch, 0)

    def reduced_rows(batch, first=0, rows=None):
        return pl.ds(REDUCED_ROW[batch] + first, BATCH_ROWS[batch] if rows is None else rows)

    def reduce_step(batch, step):
        rows = BATCH_ROWS[batch]
        for j in range(len(rounds[step - 1])):
            pair_copy(batch, step - 1, j).wait_recv()
        if step > 1:
            for way in range(2):
                red_copy(batch, way, step - 1).wait_recv()
        if step == 1:
            farthest = both_cores(batch, 0, 0).astype(BF16)
            totals = [farthest[0 : rows // 2], farthest[rows // 2 : rows]]
        elif step < 5:
            totals = [
                (both_cores(batch, step - 1, way) + arrived(batch, way, step - 1)).astype(BF16) for way in range(2)
            ]
        else:
            total = both_cores(batch, 4, 0) + arrived(batch, 0, 4) + arrived(batch, 1, 4)
            reduced[reduced_rows(batch), :] = total
        if step < 5:
            for way in range(2):
                if step > 2:
                    red_copy(batch, way, step - 2).wait_send()
                red[8 + 2 * way + step % 2, slot_rows(batch, totals[way].shape[0]), :] = totals[way]
            for way in range(2):
                red_copy(batch, way, step).start()
            send_pair(batch, step)
        else:
            for way in range(2):
                for sent in (3, 4):
                    red_copy(batch, way, sent).wait_send()
            for number, j in ((2, 1), (3, 0), (3, 1), (4, 0)):
                pair_copy(batch, number, j).wait_send()
            if batch < 2:
                for target in (sibling, after, before):
                    pl.semaphore_signal(ready.at[batch], inc=1, device_id=target, device_id_type=MESH)

            @pl.when(section == 0)
            def _():
                if batch < 2:
                    send_last(batch, batch, 0, rows)
                elif batch == 3:
                    send_last(2, 3, 128, 32)

            @pl.when(section == 1)
            def _():
                if batch >= 2:
                    send_last(batch + 1, batch, 0, 128)

    def service(loop_step, when, *steps):
        @pl.when(loop_step == when)
        def _():
            for batch, step in steps:
                reduce_step(batch, step)
                if batch == 3:
                    vec_step(step)

    def vec_line(block):
        line = jnp.concatenate(
            [
                0.5 * jnp.sum(vec[block, 0], axis=0, keepdims=True),
                0.5 * jnp.sum(vec[block, 1, :, 0:D], axis=0, keepdims=True),
                jnp.sum(vec[block, 2, :, 0:D], axis=0, keepdims=True),
                0.5 * jnp.sum(vec[block, 1, :, D : 2 * D], axis=0, keepdims=True),
            ],
            axis=1,
        )
        for row in range(8):
            sums[0, 8 * block + row : 8 * block + row + 1, :] = line[:, row * 640 : (row + 1) * 640]

    def vec_share():
        return remote(sums.at[0], sums.at[1], vec_send.at[0], vec_recv.at[0], sibling)

    def vec_copy(way, hop, arriving=0):
        step = 1 if way == 0 else -1
        src = sums.at[2 + lax.rem(ring - step * (hop - 1 + arriving) + 2 * RING, RING)]
        number = 1 + 4 * way + hop - 1
        return remote(src, src, vec_send.at[number], vec_recv.at[number], after if way == 0 else before)

    def vec_step(step):
        if step == 1:
            vec_line(0)
            vec_line(1)
            vec_share().start()
            vec_share().wait_recv()
            sums[2 + ring] = sums[0] + sums[1]
        else:
            for way in range(2):
                if step < 5 or way == 0:
                    vec_copy(way, step - 1, 1).wait_recv()
        for way in range(2):
            if step < 4 or (step == 4 and way == 0):
                vec_copy(way, step).start()

    def last_copy(number):
        first, rows = ((0, 128), (128, 96), (224, 32), (0, 128), (128, 128))[number]
        part = pl.ds(first, rows)
        return remote(cross_out.at[part], cross_in.at[part], last_send.at[number], last_recv.at[number], peer)

    def send_last(number, batch, first, rows):
        begin = (0, 128, 224, 0, 128)[number]
        cross_out[begin : begin + rows, :] = reduced[reduced_rows(batch, first, rows), :].astype(BF16)
        last_copy(number).start()

    def vec_last():
        part = pl.ds(pl.multiple_of(8 - 8 * section, 8), 8)
        return remote(sums.at[0, part], sums.at[2 + RING, pl.ds(0, 8)], last_send.at[5], last_recv.at[5], peer)

    def nothing(point, t):
        pass

    def encoder_backward(run, source, grad, t, with_grads, with_store, at):
        m = run[1]

        @pl.when(t < TILES)
        def _():
            backward_out(run, grad, t, with_grads)

        at(0, t)

        @pl.when(t >= 1)
        def _():
            backward_taps(run, t - 1, with_grads)

        at(1, t)

        @pl.when(t >= 1)
        def _():
            done = t - 1

            def store(values):
                gio_stage[done % 2] = values

            backward_in(run, source, grad, done, with_grads, store if with_store else None)
            if with_store:
                gio_copy(m, done).start()
                settle(lambda s: gio_copy(m, s), done, TILES)

        at(2, t)

    def decoder_services(point, t):
        if point == 0:
            service(t, 0, (0, 1), (1, 1))
        else:
            for step in range(2, 6):
                service(t, step - 1, (point - 1, step))

    sentence_bounds(0)
    sentence_bounds(1)

    @pl.when(section == 0)
    def _():
        def spare_slot(t, half):
            return 8 * (t // 2) + 2 * (t % 2) + half

        def spare_copy(t, half):
            src = ends.at[0, tile_rows(t), pl.ds(half * H, H)]
            return pltpu.make_async_copy(src, red.at[spare_slot(t, half), pl.ds(0, TILE)], spare_sem.at[t, half])

        def read_spare(t, cols):
            halves = [red[spare_slot(t, half), 0:TILE, :] for half in range(2) if cols.start <= half * H < cols.stop]
            return jnp.concatenate(halves, axis=1)

        def park(j, back):
            src, dst = panels[2 + j], parked.at[j]
            return pltpu.make_async_copy(*((dst, src) if back else (src, dst)), park_sem.at[j])

        for t in range(TILES):
            for half in range(2):
                spare_copy(t, half).start()

        def encoder_forward(run, read, t, staged, at):
            m = run[1]

            @pl.when(t < TILES)
            def _():
                forward_in(run, read, t, LEAD)

            at(0, t)

            @pl.when(t >= 1)
            def _():
                done = t - 1

                def store(cols, values):
                    if staged:
                        act_stage[done % 2, :, cols] = values
                    else:
                        bufs[0, tile_rows(done), cols] = values

                forward_out(run, read, done, LEAD, store)
                act_copy(m, done, staged).start()
                settle(lambda s: act_copy(m, s, staged), done, TILES)

            at(1, t)

        def late_at(*plan):
            def at(point, t):
                for when, where, hop in plan:
                    if where == point:

                        @pl.when(t == when)
                        def _():
                            finish_early() if hop == 0 else advance_late(hop)

            return at

        early_run, decoder_run, late_run = (0, 1, 0, 0), (1, 1, 1, 1), (0, 0, 1, 2)

        @steps(TILES + 1, False)
        def _(t):
            encoder_forward(early_run, reader(own), t, False, late_at((0, 0, 0), (1, 0, 1), (3, 0, 2)))

        for t in range(TILES):
            act_pass(t).start()
        for t in range(TILES):
            for half in range(2):
                spare_copy(t, half).wait()

        @steps(TILES + 1, False)
        def _(t):
            encoder_forward(late_run, read_spare, t, True, late_at((0, 0, 3), (2, 1, 4)))

        for j in range(2):
            park(j, False).start()
        for j in range(2):
            park(j, False).wait()

        @steps(TILES + 1, False)
        def _(t):
            @pl.when(t < TILES)
            def _():
                wait_raw(t)
                forward_in(decoder_run, reader(bufs.at[0]), t, LEAD)
                forward_out(decoder_run, reader(bufs.at[0]), t, LEAD, None)
                backward_out(decoder_run, bufs.at[2], t, True)

            @pl.when(t >= 1)
            def _():
                done = t - 1

                def store(values):
                    bufs[2, tile_rows(done), :] = values

                backward_taps(decoder_run, done, True)
                backward_in(decoder_run, bufs.at[0], bufs.at[2], done, True, store)

        for j in range(2):
            park(j, True).start()
        begin_reduce(0)
        begin_reduce(1)

        @steps(TILES + 1, False)
        def _(t):
            encoder_backward(early_run, own, bufs.at[2], t, True, True, decoder_services)

        load_own(0).start()
        begin_reduce(2)
        begin_reduce(3)
        load_own(0).wait()
        for j in range(2):
            park(j, True).wait()

        def backward_services(point, t):
            if point == 0:
                service(t, 0, (2, 1), (3, 1))
            else:
                for when in range(1, 4):
                    service(t, when, (point + 1, when + 1))
                if point == 1:
                    service(t, 4, (2, 5))

        @steps(TILES + 1, False)
        def _(t):
            @pl.when(t < TILES)
            def _():
                grad_pass(t).wait_recv()

            encoder_backward(late_run, own, bufs.at[1], t, False, True, backward_services)

        reduce_step(3, 5)
        vec_step(5)
        for t in range(TILES):
            act_pass(t).wait_send()

    @pl.when(section == 1)
    def _():
        encoder_run, first_run, second_run = (0, 0, 0, 0), (1, 0, 1, 1), (1, 1, 1, 1)

        def decoder_forward(run, source, t, lead, at):
            def store(cols, values):
                act_stage[t % 2, :, cols] = values

            forward_in(run, reader(source), t, lead)
            at(0, t)
            forward_out(run, reader(source), t, lead, store)
            act_copy(run[1], t, True).start()
            settle(lambda s: act_copy(run[1], s, True), t, TILES)

        @steps(TILES + 2, False)
        def _(t):
            @pl.when(t < TILES)
            def _():
                wait_raw(t)
                forward_in(encoder_run, reader(bufs.at[2]), t, LEAD)

            @pl.when(t == 0)
            def _():
                finish_early()
                advance_late(1)

            @pl.when(t == 2)
            def _():
                advance_late(3)

            @pl.when((t >= 1) & (t <= TILES))
            def _():
                done = t - 1

                def store(cols, values):
                    bufs[0, tile_rows(done), cols] = values

                forward_out(encoder_run, reader(bufs.at[2]), done, LEAD, store)

            @pl.when(t == 1)
            def _():
                advance_late(2)

            @pl.when(t == 2)
            def _():
                advance_late(4)

            @steps(2, False)
            def _(second):
                @pl.when((t >= 2) & (t <= TILES) & ((second == 1) | (t == 2)))
                def _():
                    done = t - 2 + second
                    decoder_forward(first_run, bufs.at[0], done, LEAD - TILE, nothing)
                    backward_out(first_run, own, done, True)

            @pl.when(t >= 2)
            def _():
                done = t - 2

                def store(values):
                    gio_stage[done % 2] = values
                    own[tile_rows(done), :] = values

                backward_taps(first_run, done, True)
                backward_in(first_run, bufs.at[0], own, done, True, store)
                gio_copy(0, done).start()
                settle(lambda s: gio_copy(0, s), done, TILES)

                @pl.when(done >= 1)
                def _():
                    grad_pass(done - 1).start()

        grad_pass(TILES - 1).start()
        begin_reduce(0)
        begin_reduce(1)

        @steps(TILES + 1, False)
        def _(t):
            encoder_backward(encoder_run, bufs.at[2], own, t, True, False, decoder_services)

        load_own(1).start()
        begin_reduce(2)
        begin_reduce(3)
        load_own(1).wait()

        def encoder_services(point, t):
            if point == 0:
                service(t, 0, (2, 1), (3, 1))
                for when in range(1, 4):
                    service(t, when, (3, when + 1))
            elif point == 1:
                for when in range(0, 4):
                    service(t, when, (2, when + 2))
            else:
                service(t, 3, (3, 5))

        @steps(TILES + 1, False)
        def _(t):
            @pl.when(t < TILES)
            def _():
                act_pass(t).wait_recv()
                decoder_forward(second_run, bufs.at[1], t, LEAD, encoder_services)
                backward_out(second_run, own, t, False)

            encoder_services(1, t)

            @pl.when(t >= 1)
            def _():
                done = t - 1

                def store(values):
                    gio_stage[done % 2] = values

                backward_taps(second_run, done, False)
                backward_in(second_run, bufs.at[1], own, done, False, store)
                gio_copy(1, done).start()
                settle(lambda s: gio_copy(1, s), done, TILES)

            encoder_services(2, t)

        for t in range(TILES):
            grad_pass(t).wait_send()

    vec_share().wait_send()
    total = sums[2]
    for chip_sum in range(1, RING):
        total = total + sums[2 + chip_sum]
    sums[0] = total
    vec_last().start()

    @pl.when(section == 0)
    def _():
        last_copy(3).wait_recv()
        last_copy(4).wait_recv()
        terms = [reduced[reduced_rows(2), :], reduced[reduced_rows(3, 0, 128), :]]
        total = jnp.concatenate(terms, axis=0) + cross_in[...].astype(F32)
        grads_out[...] = jnp.concatenate([total[128:192], total[0:128], total[192:256]], axis=0)

    @pl.when(section == 1)
    def _():
        for number in range(3):
            last_copy(number).wait_recv()
        terms = [reduced[reduced_rows(0), :], reduced[reduced_rows(1), :], reduced[reduced_rows(3, 128, 32), :]]
        grads_out[...] = jnp.concatenate(terms, axis=0) + cross_in[...].astype(F32)

    vec_last().wait_recv()
    line = sums[0, pl.ds(pl.multiple_of(8 * section, 8), 8), :] + sums[2 + RING, 0:8, :]
    line_out[...] = line

    for part in range(5):
        for hop in range(1, 5):
            for way in range(2):
                ring_copy(part, hop, way).wait_send()
        share_copy(part, ring, 0, core).wait_send()
        for slot in range(1, 8):
            share_copy(part, ring, slot, core).wait_send()
    for half in range(2):
        cross_copy(half, section).wait_send()
    for copy in cross_params(section):
        copy.wait_send()
    for number in range(2 * TILES):
        raw_copy(number).wait_send()
    for way in range(2):
        for hop in range(1, 5 if way == 0 else 4):
            vec_copy(way, hop).wait_send()
    vec_last().wait_send()

    @pl.when(section == 0)
    def _():
        for number in range(3):
            last_copy(number).wait_send()

    @pl.when(section == 1)
    def _():
        for number in range(3, 5):
            last_copy(number).wait_send()


def finish_kernel(
    act, gio, grads, line, act_out, gio_out, in_out, out_out, tap_out, gain_out, bias_out, act_buf, gio_buf, wide, sems
):
    count, rows = act_buf.shape[:2]

    def part(ref, i):
        return ref.at[pl.ds(i * rows, rows)]

    def gio_in(i):
        return pltpu.make_async_copy(part(gio, i), gio_buf.at[i], sems.at[0, i])

    def act_in(i):
        return pltpu.make_async_copy(part(act, i), act_buf.at[i], sems.at[1, i])

    def gio_back(i):
        return pltpu.make_async_copy(wide.at[i], part(gio_out, i), sems.at[2, i])

    def act_back(i):
        return pltpu.make_async_copy(act_buf.at[i], part(act_out, i), sems.at[3, i])

    for i in range(count):
        gio_in(i).start()
        act_in(i).start()
    for i in range(count):
        act_in(i).wait()
        act_back(i).start()
        gio_in(i).wait()
        wide[i] = gio_buf[i].astype(F32)
        gio_back(i).start()
        for r in range(64 * i // count, 64 * (i + 1) // count):
            in_out[:, r * H : (r + 1) * H] = grads[r : r + 1, :]
        for r in range(32 * i // count, 32 * (i + 1) // count):
            for half in range(2):
                row = 64 + 32 * half + r
                out_out[:, (2 * r + half) * H : (2 * r + half + 1) * H] = grads[row : row + 1, :]
            for number, slot in enumerate((1, 2, 3, 0)):
                row = 128 + 32 * number + r
                tap_out[slot : slot + 1, r * H : (r + 1) * H] = grads[row : row + 1, :]
    flat = jnp.concatenate([line[row : row + 1, :] for row in range(8)], axis=1)
    gain_out[...] = flat[:, 0 : 2 * D]
    bias_out[...] = flat[:, 2 * D : 5 * D]
    for i in range(count):
        act_back(i).wait()
        gio_back(i).wait()


def finish(act, gio, grads, line):
    micro, rows = act.shape[:2]
    flat = (micro * rows, D)
    count = 4
    block = (count, micro * rows // count, D)
    shape = jax.ShapeDtypeStruct
    hbm = pl.BlockSpec(memory_space=pl.ANY)
    whole = pl.BlockSpec(memory_space=pltpu.VMEM)
    act, gio, *rest = pl.pallas_call(
        finish_kernel,
        out_shape=[
            shape(flat, BF16),
            shape(flat, F32),
            shape((1, 64 * H), F32),
            shape((1, 64 * H), F32),
            shape((4, 32 * H), F32),
            shape((1, 2 * D), F32),
            shape((1, 3 * D), F32),
        ],
        in_specs=[hbm, hbm, whole, whole],
        out_specs=[hbm, hbm] + [whole] * 5,
        scratch_shapes=[
            pltpu.VMEM(block, BF16),
            pltpu.VMEM(block, BF16),
            pltpu.VMEM(block, F32),
            pltpu.SemaphoreType.DMA((4, count)),
        ],
        compiler_params=pltpu.CompilerParams(vmem_limit_bytes=64 << 20),
        name="finish",
    )(act.reshape(flat), gio.reshape(flat), grads, line)
    return (act.reshape(micro, rows, D), gio.reshape(micro, rows, D), *rest)


def local(group, block_ends, proj_in, proj_out, conv_taps, norm_gains, bias_terms, lengths, dilation):
    micro, rows = block_ends.shape[1:3]
    if group > 1:
        proj_in = lax.all_gather(proj_in, "lane", axis=1, tiled=True)
        proj_out = lax.all_gather(proj_out, "lane", axis=1, tiled=True)
        conv_taps = lax.all_gather(conv_taps, "lane", axis=2, tiled=True)
    vmem = pl.BlockSpec(memory_space=pltpu.VMEM)
    smem = pl.BlockSpec(memory_space=pltpu.SMEM)
    hbm = pl.BlockSpec(memory_space=pl.ANY)
    shape = jax.ShapeDtypeStruct
    dma = pltpu.SemaphoreType.DMA
    act, gio, grads, line, _ = pl.pallas_call(
        functools.partial(kernel, group),
        out_shape=[
            shape((micro, rows, D), BF16),
            shape((micro, rows, D), BF16),
            shape((256, H), F32),
            shape((8, 640), F32),
            shape((2, PANELS, LEN + 2 * PAD, LANES), F32),
        ],
        in_specs=[smem, smem, hbm, vmem, vmem, vmem, vmem, vmem],
        out_specs=[hbm, hbm, vmem, vmem, hbm],
        scratch_shapes=[
            pltpu.VMEM((2 * POSITIONS * PIECE, H), BF16),
            pltpu.VMEM((LEN, D), BF16),
            pltpu.VMEM((3, LEN, D), BF16),
            *[pltpu.VMEM((PANELS, LEN + 2 * PAD, LANES), F32) for _ in range(4)],
            pltpu.VMEM((PANELS, LEAD + LEN + PAD, LANES), F32),
            pltpu.VMEM((3, LEN, LANES), F32),
            pltpu.VMEM((2, LEN, LANES), jnp.int32),
            pltpu.VMEM((ACC_ROWS, H), F32),
            pltpu.VMEM((2, 3, 8, 2 * D), F32),
            pltpu.VMEM((2, TILE, D), BF16),
            pltpu.VMEM((2, TILE, D), BF16),
            pltpu.VMEM((2, 1, 2 * D), F32),
            pltpu.VMEM((2, 1, 3 * D), F32),
            pltpu.VMEM((3 + RING, 16, 640), F32),
            pltpu.VMEM((16, MOST, H), BF16),
            pltpu.VMEM((REDUCED, H), F32),
            pltpu.VMEM((256, H), BF16),
            pltpu.VMEM((256, H), BF16),
            pltpu.VMEM((PIECE, H), BF16),
            pltpu.VMEM((TILE, H), BF16),
            dma((2, 5, 4)),
            dma((2, 5, 4)),
            dma((5, 8)),
            dma((5, 8)),
            dma((4,)),
            dma((4,)),
            dma((2 * TILES,)),
            dma((2 * TILES,)),
            dma((TILES,)),
            dma((TILES,)),
            dma((5,)),
            dma((TILES, 2)),
            dma((2,)),
            dma((2,)),
            dma((2,)),
            dma((4, 2, 4)),
            dma((4, 2, 4)),
            dma((4, 5, 2)),
            dma((4, 5, 2)),
            dma((9,)),
            dma((9,)),
            dma((6,)),
            dma((6,)),
            pltpu.SemaphoreType.REGULAR((2,)),
        ],
        compiler_params=pltpu.CompilerParams(
            collective_id=0, has_side_effects=True, vmem_limit_bytes=64 << 20
        ),
        name="residual_blocks",
    )(dilation, lengths[:, 0, :], block_ends[0], proj_in, proj_out, conv_taps[0], norm_gains, bias_terms)
    act, gio, *grads, gain_sum, bias_sum = finish(act, gio, grads, line)
    grads[2] = grads[2][None]
    if group > 1:
        grads = tuple(
            lax.psum_scatter(part, "lane", scatter_dimension=part.ndim - 1, tiled=True) for part in grads
        )
        gain_sum, bias_sum = lax.psum((gain_sum, bias_sum), "lane")
    return (act[None], gio[None], *grads, gain_sum, bias_sum)


def solution(mesh):
    group = mesh.shape["dp"] // POSITIONS
    spread = "dp"
    if group > 1:
        mesh = Mesh(mesh.devices.reshape(2, POSITIONS, group), ("section", "dp", "lane"))
        spread = ("dp", "lane")
    placed = (
        P("section", None, spread, None),
        P("section", spread),
        P("section", spread),
        P("section", None, spread),
        P("section", None),
        P("section", None),
        P(None, spread, None),
        P(),
    )
    return jax.shard_map(
        functools.partial(local, group),
        mesh=mesh,
        in_specs=placed,
        out_specs=(
            P("section", None, spread, None),
            P("section", None, spread, None),
            P("section", spread),
            P("section", spread),
            P("section", None, spread),
            P("section", None),
            P("section", None),
        ),
        check_vma=False,
    )
```

```python
import functools

import jax
import jax.numpy as jnp
from jax import lax
from jax.experimental import pallas as pl
from jax.experimental.pallas import tpu as pltpu
from jax.sharding import Mesh
from jax.sharding import PartitionSpec as P

D = 1024
H = 512
LEN = 1024
POSITIONS = 16
RING = 8
TILE = 256
TILES = LEN // TILE
PAD = 128
CHUNK = 256
LANES = 128
PANELS = H // LANES
epsilon = 1e-05
linear_term = 0.7978845608028654
cubic_term = linear_term * 0.044715
kappa = cubic_term ** (1.0 / 3.0)
beta = linear_term / kappa
MESH = pl.DeviceIdType.MESH
F32 = jnp.float32
BF16 = jnp.bfloat16

PIECE = 256
EARLY = ((0, 0, 96), (0, 96, 160), (1, 0, 32))
LATE = ((1, 32, 64), (1, 96, 160))
PARTS = EARLY + LATE
TAPS = (5, 3)
ACC_BASE = (0, 2 * D + 5 * H)
ACC_ROWS = 4 * D + 8 * H
BATCHES = (
    (1, ((0, 64), (D, 32), (D + H, 32))),
    (1, ((2 * D, 32), (2 * D + H, 32), (2 * D + 2 * H, 32))),
    (0, ((D, 32), (D + H, 32), (2 * D + H, 32), (2 * D + 2 * H, 32))),
    (0, ((0, 64), (2 * D + 3 * H, 32), (2 * D, 32), (2 * D + 4 * H, 32))),
)
BATCH_ROWS = (128, 96, 128, 160)
SLOT_ROW = (0, 128, 0, 128)
REDUCED_ROW = (0, 128, 224, 352)
REDUCED = 512
MOST = 288
LEAD = 384


def aligned(start, size):
    return start if isinstance(start, int) else pl.multiple_of(start, size)


def steps(count, unroll):
    def run(body):
        if not unroll:
            return pl.loop(0, count)(body)
        for t in range(count):
            body(t)

    return run


def product(left, right):
    return jnp.dot(left, right, preferred_element_type=F32)


def contract_rows(left, right):
    return lax.dot_general(left, right, (((0,), (0,)), ((), ())), preferred_element_type=F32)


def contract_columns(left, right):
    return lax.dot_general(left, right, (((1,), (1,)), ((), ())), preferred_element_type=F32)


def normalise(values):
    mean = jnp.mean(values, axis=-1, keepdims=True)
    centre = values - mean
    scale = lax.rsqrt(jnp.mean(centre * centre, axis=-1, keepdims=True) + epsilon)
    return centre * scale, mean, scale


def gelu(normal, gain, bias):
    half = normal * (0.5 * gain) + 0.5 * bias
    inner = half * (half * half * (8.0 * cubic_term) + 2.0 * linear_term)
    return half + half * jnp.tanh(inner)


def gelu_parts(normal, gain, bias):
    arg = normal * (kappa * gain) + kappa * bias
    square = arg * arg
    rise = 1.0 + jnp.tanh(arg * (square + beta))
    double_slope = rise * (1.0 + (2.0 - rise) * (arg * (3.0 * square + beta)))
    return arg, rise, double_slope


def gelu_again(arg, rise):
    return (arg * rise * (0.5 / kappa)).astype(BF16)


def norm_back(normal, scale, gain, double_q):
    weighted = (0.5 * gain) * double_q
    count = 1.0 / normal.shape[-1]
    mean = jnp.sum(weighted, axis=-1, keepdims=True) * count
    along = jnp.sum(weighted * normal, axis=-1, keepdims=True) * count
    return (weighted - mean - normal * along) * scale


def fold_rows(values):
    return jnp.sum(values.reshape(values.shape[0] // 8, 8, values.shape[1]), axis=0)


def ring_chip(place):
    place = lax.rem(place + 2 * RING, RING)
    return jnp.where(place < RING // 2, 2 * place, 2 * (RING - place) - 1)


def kernel(group, dilation, lengths, ends, proj_in, proj_out, conv_taps, gains, biases, *refs):
    (
        act_out,
        gio_out,
        grads_out,
        line_out,
        parked,
        weights,
        own,
        bufs,
        panel_0,
        panel_1,
        panel_2,
        panel_3,
        shift,
        stats,
        bounds,
        acc,
        vec,
        gio_stage,
        act_stage,
        all_gains,
        all_biases,
        sums,
        red,
        reduced,
        cross_out,
        cross_in,
        piece,
        middle,
        ring_send,
        ring_recv,
        sib_send,
        sib_recv,
        cross_send,
        cross_recv,
        raw_send,
        raw_recv,
        pass_send,
        pass_recv,
        local_sem,
        spare_sem,
        park_sem,
        act_sem,
        gio_sem,
        red_send,
        red_recv,
        pair_send,
        pair_recv,
        vec_send,
        vec_recv,
        last_send,
        last_recv,
        ready,
    ) = refs
    panels = (panel_0, panel_1, panel_2, panel_3)
    section = lax.axis_index("section")
    index = lax.axis_index("dp")
    place, lane = index // group, lax.rem(index, group)
    chip, core = place // 2, lax.rem(place, 2)
    ring = jnp.where(lax.rem(chip, 2) == 0, chip // 2, RING - (chip + 1) // 2)

    def device(sec, position):
        return {"section": sec, "dp": position * group + lane}

    def position(ring_place, which_core):
        return 2 * ring_chip(ring_place) + which_core

    peer = device(1 - section, place)
    sibling = device(section, 2 * chip + 1 - core)
    after = device(section, position(ring + 1, core))
    before = device(section, position(ring - 1, core))

    def remote(src, dst, send, recv, target):
        return pltpu.make_async_remote_copy(
            src_ref=src, dst_ref=dst, send_sem=send, recv_sem=recv, device_id=target, device_id_type=MESH
        )

    barrier = pltpu.get_barrier_semaphore()
    for target in (peer, sibling, after, before):
        pl.semaphore_signal(barrier, inc=1, device_id=target, device_id_type=MESH)
    def lay_out(row, values):
        reduced[row : row + 1, :] = values.astype(F32)

    for r in range(32):
        lay_out(r, conv_taps[0:1, r * H : (r + 1) * H])
    for r in range(64):
        lay_out(32 + r, proj_in[0:1, r * H : (r + 1) * H])
    piece[0:96, :] = reduced[0:96, :].astype(BF16)
    pl.semaphore_wait(barrier, 4)

    def rows_of(part, origin, half=None):
        sec, first, rows = PARTS[part]
        if half is not None:
            first, rows = first + half * (rows // 2), rows // 2
        return pl.ds(pl.multiple_of((sec * POSITIONS + origin) * PIECE + first, 16), rows)

    def ring_copy(part, hop, way):
        step = 1 if way == 0 else -1
        rows = rows_of(part, position(ring - step * (hop - 1), core), way if hop == 4 else None)
        return remote(
            weights.at[rows], weights.at[rows], ring_send.at[way, part, hop - 1], ring_recv.at[way, part, hop - 1],
            after if way == 0 else before,
        )

    def ring_arrival(part, hop, way):
        step = 1 if way == 0 else -1
        rows = rows_of(part, position(ring - step * hop, core), way if hop == 4 else None)
        return remote(
            weights.at[rows], weights.at[rows], ring_send.at[way, part, hop - 1], ring_recv.at[way, part, hop - 1],
            after if way == 0 else before,
        )

    def share_copy(part, ring_place, slot, which_core):
        rows = rows_of(part, position(ring_place, which_core))
        return remote(
            weights.at[rows], weights.at[rows], sib_send.at[part, slot], sib_recv.at[part, slot], sibling
        )

    def start_part(part):
        for way in range(2):
            ring_copy(part, 1, way).start()
        share_copy(part, ring, 0, core).start()

    def advance(part, hop):
        for way in range(2):
            ring_arrival(part, hop, way).wait_recv()
            if hop < 4:
                ring_copy(part, hop + 1, way).start()
                share_copy(part, ring - hop if way == 0 else ring + hop, 2 * hop - 1 + way, core).start()
        if hop == 4:
            share_copy(part, ring + 4, 7, core).start()

    def wait_shared(parts):
        for part in parts:
            share_copy(part, ring, 0, 1 - core).wait_recv()
            for hop in range(1, 4):
                for way in range(2):
                    share_copy(part, ring - hop if way == 0 else ring + hop, 2 * hop - 1 + way, 1 - core).wait_recv()
            share_copy(part, ring + 4, 7, 1 - core).wait_recv()

    def cross_copy(half, sec):
        first, rows = ((0, 96), (96, 160))[half]
        slot = pl.ds(pl.multiple_of((sec * POSITIONS + place) * PIECE + first, 16), rows)
        return remote(piece.at[pl.ds(first, rows)], weights.at[slot], cross_send.at[half], cross_recv.at[half], peer)

    def cross_params(sec):
        return (
            remote(gains, all_gains.at[sec], cross_send.at[2], cross_recv.at[2], peer),
            remote(biases, all_biases.at[sec], cross_send.at[3], cross_recv.at[3], peer),
        )

    def tile_rows(t):
        return pl.ds(aligned(t * TILE, TILE), TILE)

    def raw_copy(number):
        rows = pl.ds(aligned(number * (TILE // 2), TILE // 2), TILE // 2)
        return remote(ends.at[section, rows], bufs.at[2, rows], raw_send.at[number], raw_recv.at[number], peer)

    def wait_raw(t):
        for half in range(2):
            raw_copy(2 * t + half).wait_recv()

    def own_slot(half):
        first, rows = ((0, 96), (96, 160))[half]
        slot = pl.ds(pl.multiple_of((section * POSITIONS + place) * PIECE + first, 16), rows)
        return pltpu.make_async_copy(piece.at[pl.ds(first, rows)], weights.at[slot], local_sem.at[0 if half == 0 else 4])

    keep_gains = pltpu.make_async_copy(gains, all_gains.at[section], local_sem.at[1])
    keep_biases = pltpu.make_async_copy(biases, all_biases.at[section], local_sem.at[3])

    def load_own(m):
        return pltpu.make_async_copy(ends.at[m], own, local_sem.at[2])

    cross_copy(0, section).start()
    own_slot(0).start()
    own_slot(0).wait()

    @pl.when(section == 0)
    def _():
        start_part(0)

    @pl.when(section == 1)
    def _():
        start_part(2)

    for r in range(32):
        for half in range(2):
            first = (2 * r + half) * H
            lay_out(96 + 32 * half + r, proj_out[0:1, first : first + H])
        for slot in range(1, 4):
            lay_out(128 + 32 * slot + r, conv_taps[slot : slot + 1, r * H : (r + 1) * H])
    piece[96:PIECE, :] = reduced[96:PIECE, :].astype(BF16)
    cross_copy(1, section).start()
    own_slot(1).start()
    for copy in cross_params(section):
        copy.start()
    for number in range(2 * TILES):
        raw_copy(number).start()
    keep_gains.start()
    keep_biases.start()
    load_own(1 - section).start()
    own_slot(1).wait()

    @pl.when(section == 0)
    def _():
        start_part(1)

    acc[...] = jnp.zeros_like(acc)
    vec[...] = jnp.zeros_like(vec)
    cross_copy(0, 1 - section).wait_recv()

    @pl.when(section == 0)
    def _():
        start_part(2)

    @pl.when(section == 1)
    def _():
        start_part(0)

    cross_copy(1, 1 - section).wait_recv()

    @pl.when(section == 1)
    def _():
        start_part(1)

    for hop in range(1, 4):
        for part in range(3):
            advance(part, hop)
    start_part(3)
    advance(0, 4)
    start_part(4)
    wait_shared([0])
    keep_gains.wait()
    keep_biases.wait()
    load_own(1 - section).wait()
    for copy in cross_params(1 - section):
        copy.wait_recv()

    def finish_early():
        for part in range(1, 3):
            advance(part, 4)
        wait_shared(range(1, 3))

    def advance_late(hop):
        for part in range(3, 5):
            advance(part, hop)
        if hop == 4:
            wait_shared(range(3, 5))

    def matrix(sec, first, rows):
        starts = [(sec * POSITIONS + pos) * PIECE + first for pos in range(POSITIONS)]
        return jnp.concatenate([weights[start : start + rows, :] for start in starts], axis=0)

    def weight_in(block):
        return matrix(block, 32, 64)

    def weight_out(block, half):
        return matrix(block, 96 + 32 * half, 32)

    def tap(block, k):
        sec, slot = (0, k) if block == 0 and k < 4 else (1, 0) if block == 0 else (1, k + 1)
        return matrix(sec, 0 if slot == 0 else 128 + 32 * slot, 32)

    def gain(block, norm):
        first, size = ((0, D), (D, H), (D + H, H))[norm]
        return all_gains[block, :, first : first + size]

    def bias(block, norm):
        first, size = ((0, D), (2 * D, H), (2 * D + H, H))[norm]
        return all_biases[block, :, first : first + size]

    def out_bias(block, half):
        first = D + half * H
        return all_biases[block, :, first : first + H]

    def put_panels(which, base, values):
        for j in range(PANELS):
            panels[which][j, pl.ds(PAD + base, TILE), :] = values[:, j * LANES : (j + 1) * LANES]

    def get_panels(which, start):
        return jnp.concatenate([panels[which][j, pl.ds(start, TILE), :] for j in range(PANELS)], axis=1)

    def put_shift(lead, base, values):
        for j in range(PANELS):
            shift[j, pl.ds(lead + base, TILE), :] = values[:, j * LANES : (j + 1) * LANES]

    def get_shift(start):
        return jnp.concatenate([shift[j, pl.ds(start, TILE), :] for j in range(PANELS)], axis=1)

    def reach(m, base):
        packed = bounds[m, pl.ds(base, TILE), :]
        return -(packed & (LEN - 1)), packed >> 10

    def masked(limits, values, offset):
        inside = (offset >= limits[0]) & (offset <= limits[1])
        return jnp.where(jnp.concatenate([inside] * PANELS, axis=1), values, 0.0).astype(BF16)

    def sentence_bounds(m):
        row = lax.broadcasted_iota(jnp.int32, (LEN, LANES), 0)
        first = jnp.zeros((LEN, LANES), jnp.int32)
        last = jnp.full((LEN, LANES), LEN, jnp.int32)
        reached = jnp.int32(0)
        for j in range(8):
            end = reached + lengths[m, j]
            inside = (row >= reached) & (row < end)
            first = jnp.where(inside, reached, first)
            last = jnp.where(inside, end, last)
            reached = end
        bounds[m] = (last - 1 - row) * LEN + row - first

    def add_product(block, first, act, grad):
        for begin in range(0, act.shape[1], CHUNK):
            rows = pl.ds(ACC_BASE[block] + first + begin, CHUNK)
            acc[rows, :] += contract_rows(act[:, begin : begin + CHUNK], grad)

    def forward_in(run, read, t, lead):
        block, _, pair, stat = run
        base = aligned(t * TILE, TILE)
        rows = pl.ds(base, TILE)
        normal, mean, scale = normalise(read(t, slice(0, D)).astype(F32))
        stats[stat, rows, 0:1] = mean
        stats[stat, rows, 1:2] = scale
        act = gelu(normal, gain(block, 0), bias(block, 0)).astype(BF16)
        normal, _, scale = normalise(product(act, weight_in(block)))
        stats[stat, rows, 2:3] = scale
        put_panels(2 * pair, base, normal)
        act = gelu(normal, gain(block, 1), bias(block, 1)).astype(BF16)
        put_shift(lead, base, act.astype(F32))

    def forward_out(run, read, t, lead, store):
        block, m, pair, stat = run
        base = aligned(t * TILE, TILE)
        rows = pl.ds(base, TILE)
        limits = reach(m, base)
        conv = None
        for k in range(TAPS[block]):
            offset = (k - 2) * dilation[block]
            term = product(masked(limits, get_shift(lead + base + offset), offset), tap(block, k))
            conv = term if conv is None else conv + term
        normal, _, scale = normalise(conv)
        stats[stat, rows, 3:4] = scale
        put_panels(2 * pair + 1, base, normal)
        if store is None:
            return
        act = gelu(normal, gain(block, 2), bias(block, 2)).astype(BF16)
        for half in range(2):
            cols = slice(half * H, (half + 1) * H)
            residual = read(t, cols).astype(F32) + product(act, weight_out(block, half))
            store(cols, (residual + out_bias(block, half)).astype(BF16))

    def backward_out(run, grad, t, with_grads):
        block, _, pair, stat = run
        base = aligned(t * TILE, TILE)
        rows = pl.ds(base, TILE)
        upstream = contract_columns(grad[rows, 0:H], weight_out(block, 0))
        upstream = upstream + contract_columns(grad[rows, H:D], weight_out(block, 1))
        normal = get_panels(2 * pair + 1, PAD + base)
        arg, rise, double_slope = gelu_parts(normal, gain(block, 2), bias(block, 2))
        double_q = upstream * double_slope
        if with_grads:
            vec[block, 0, :, D + H : 2 * D] += fold_rows(double_q * normal)
            vec[block, 1, :, D + H : 2 * D] += fold_rows(double_q)
            vec[block, 2, :, 0:D] += fold_rows(grad[rows, :].astype(F32))
            act = gelu_again(arg, rise)
            for half in range(2):
                add_product(block, D + half * H, act, grad[rows, half * H : (half + 1) * H])
        back = norm_back(normal, stats[stat, rows, 3:4], gain(block, 2), double_q)
        put_panels(2 * pair + 1, base, back.astype(BF16).astype(F32))

    def backward_taps(run, t, with_grads):
        block, m, pair, stat = run
        base = aligned(t * TILE, TILE)
        rows = pl.ds(base, TILE)
        normal = get_panels(2 * pair, PAD + base)
        arg, rise, double_slope = gelu_parts(normal, gain(block, 1), bias(block, 1))
        if with_grads:
            act = gelu_again(arg, rise)
        limits = reach(m, base)
        upstream = None
        for k in range(TAPS[block]):
            offset = (2 - k) * dilation[block]
            moved = masked(limits, get_panels(2 * pair + 1, PAD + base + offset), offset)
            term = contract_columns(moved, tap(block, k))
            upstream = term if upstream is None else upstream + term
            if with_grads:
                add_product(block, 2 * D + k * H, act, moved)
        double_q = upstream * double_slope
        if with_grads:
            vec[block, 0, :, D : D + H] += fold_rows(double_q * normal)
            vec[block, 1, :, D : D + H] += fold_rows(double_q)
        middle[...] = norm_back(normal, stats[stat, rows, 2:3], gain(block, 1), double_q).astype(BF16)

    def backward_in(run, source, grad, t, with_grads, store):
        block, _, _, stat = run
        base = aligned(t * TILE, TILE)
        rows = pl.ds(base, TILE)
        back = middle[...]
        upstream = contract_columns(back, weight_in(block))
        scale = stats[stat, rows, 1:2]
        normal = (source[rows, :].astype(F32) - stats[stat, rows, 0:1]) * scale
        arg, rise, double_slope = gelu_parts(normal, gain(block, 0), bias(block, 0))
        double_q = upstream * double_slope
        if with_grads:
            add_product(block, 0, gelu_again(arg, rise), back)
            vec[block, 0, :, 0:D] += fold_rows(double_q * normal)
            vec[block, 1, :, 0:D] += fold_rows(double_q)
        if store is not None:
            store((grad[rows, :].astype(F32) + norm_back(normal, scale, gain(block, 0), double_q)).astype(BF16))

    def reader(ref):
        return lambda t, cols: ref[tile_rows(t), cols]

    def act_copy(m, t, staged):
        src = act_stage.at[t % 2] if staged else bufs.at[0, tile_rows(t)]
        return pltpu.make_async_copy(src, act_out.at[m, tile_rows(t)], act_sem.at[t % 2])

    def gio_copy(m, t):
        slot = t % 2
        return pltpu.make_async_copy(gio_stage.at[slot], gio_out.at[m, tile_rows(t)], gio_sem.at[slot])

    def act_pass(t):
        return remote(
            act_out.at[1, tile_rows(t)], bufs.at[1, tile_rows(t)], pass_send.at[t], pass_recv.at[t], peer
        )

    def grad_pass(t):
        return remote(
            gio_out.at[0, tile_rows(t)], bufs.at[1, tile_rows(t)], pass_send.at[t], pass_recv.at[t], peer
        )

    def settle(copy, t, count):
        @pl.when(t >= 1)
        def _():
            copy(t - 1).wait()

        @pl.when(t == count - 1)
        def _():
            copy(t).wait()

    def own_piece(batch, pos):
        block, parts = BATCHES[batch]
        places = [(ACC_BASE[block] + first + size * pos, size) for first, size in parts]
        return jnp.concatenate(
            [acc[pl.ds(pl.multiple_of(first, 32), size), :] for first, size in places], axis=0
        )

    def slot_rows(batch, rows=None):
        return pl.ds(SLOT_ROW[batch], BATCH_ROWS[batch] if rows is None else rows)

    rounds = ((4,), (3, 5), (2, 6), (1, 7), (0,))

    def pair_copy(batch, number):
        count = len(rounds[number])
        src = red.at[pl.ds(2 * (number % 2), count), slot_rows(batch)]
        dst = red.at[pl.ds(4 + 2 * (number % 2), count), slot_rows(batch)]
        return remote(src, dst, pair_send.at[batch, number], pair_recv.at[batch, number], sibling)

    def send_pair(batch, number):
        if number >= 2:
            pair_copy(batch, number - 2).wait_send()
        for j, slot in enumerate(rounds[number]):
            rows = own_piece(batch, position(ring + slot, 1 - core))
            red[2 * (number % 2) + j, slot_rows(batch), :] = rows.astype(BF16)
        pair_copy(batch, number).start()

    def red_copy(batch, way, step):
        rows = slot_rows(batch, BATCH_ROWS[batch] // 2 if step == 1 else None)
        src = red.at[8 + 2 * way + step % 2, rows]
        dst = red.at[12 + 2 * way + step % 2, rows]
        target = after if way == 0 else before
        return remote(src, dst, red_send.at[batch, way, step - 1], red_recv.at[batch, way, step - 1], target)

    def both_cores(batch, number, j):
        pos = position(ring + rounds[number][j], core)
        return own_piece(batch, pos) + red[4 + 2 * (number % 2) + j, slot_rows(batch), :].astype(F32)

    def arrived(batch, way, step):
        rows = BATCH_ROWS[batch]
        if step == 1:
            half = red[12 + 2 * way + 1, slot_rows(batch, rows // 2), :].astype(F32)
            blank = jnp.zeros((rows // 2, H), F32)
            return jnp.concatenate([half, blank] if way == 0 else [blank, half], axis=0)
        return red[12 + 2 * way + step % 2, slot_rows(batch), :].astype(F32)

    def begin_reduce(batch):
        if batch >= 2:
            pl.semaphore_wait(ready.at[batch - 2], 3)
        send_pair(batch, 0)

    def reduced_rows(batch, first=0, rows=None):
        return pl.ds(REDUCED_ROW[batch] + first, BATCH_ROWS[batch] if rows is None else rows)

    def reduce_step(batch, step):
        rows = BATCH_ROWS[batch]
        pair_copy(batch, step - 1).wait_recv()
        if step > 1:
            for way in range(2):
                red_copy(batch, way, step - 1).wait_recv()
        if step == 1:
            farthest = both_cores(batch, 0, 0).astype(BF16)
            totals = [farthest[0 : rows // 2], farthest[rows // 2 : rows]]
        elif step < 5:
            totals = [
                (both_cores(batch, step - 1, way) + arrived(batch, way, step - 1)).astype(BF16) for way in range(2)
            ]
        else:
            total = both_cores(batch, 4, 0) + arrived(batch, 0, 4) + arrived(batch, 1, 4)
            reduced[reduced_rows(batch), :] = total
        if step < 5:
            for way in range(2):
                if step > 2:
                    red_copy(batch, way, step - 2).wait_send()
                red[8 + 2 * way + step % 2, slot_rows(batch, totals[way].shape[0]), :] = totals[way]
            for way in range(2):
                red_copy(batch, way, step).start()
            send_pair(batch, step)
        else:
            for way in range(2):
                for sent in (3, 4):
                    red_copy(batch, way, sent).wait_send()
            for number in (3, 4):
                pair_copy(batch, number).wait_send()
            if batch < 2:
                for target in (sibling, after, before):
                    pl.semaphore_signal(ready.at[batch], inc=1, device_id=target, device_id_type=MESH)

            @pl.when(section == 0)
            def _():
                if batch < 2:
                    send_last(batch, batch, 0, rows)
                elif batch == 3:
                    send_last(2, 3, 128, 32)

            @pl.when(section == 1)
            def _():
                if batch >= 2:
                    send_last(batch + 1, batch, 0, 128)

    def service(loop_step, when, *steps):
        @pl.when(loop_step == when)
        def _():
            for batch, step in steps:
                reduce_step(batch, step)
                if batch == 3:
                    vec_step(step)

    def vec_line(block):
        line = jnp.concatenate(
            [
                0.5 * jnp.sum(vec[block, 0], axis=0, keepdims=True),
                0.5 * jnp.sum(vec[block, 1, :, 0:D], axis=0, keepdims=True),
                jnp.sum(vec[block, 2, :, 0:D], axis=0, keepdims=True),
                0.5 * jnp.sum(vec[block, 1, :, D : 2 * D], axis=0, keepdims=True),
            ],
            axis=1,
        )
        for row in range(8):
            sums[0, 8 * block + row : 8 * block + row + 1, :] = line[:, row * 640 : (row + 1) * 640]

    def vec_share():
        return remote(sums.at[0], sums.at[1], vec_send.at[0], vec_recv.at[0], sibling)

    def vec_copy(way, hop, arriving=0):
        step = 1 if way == 0 else -1
        src = sums.at[2 + lax.rem(ring - step * (hop - 1 + arriving) + 2 * RING, RING)]
        number = 1 + 4 * way + hop - 1
        return remote(src, src, vec_send.at[number], vec_recv.at[number], after if way == 0 else before)

    def vec_step(step):
        if step == 1:
            vec_line(0)
            vec_line(1)
            vec_share().start()
            vec_share().wait_recv()
            sums[2 + ring] = sums[0] + sums[1]
        else:
            for way in range(2):
                if step < 5 or way == 0:
                    vec_copy(way, step - 1, 1).wait_recv()
        for way in range(2):
            if step < 4 or (step == 4 and way == 0):
                vec_copy(way, step).start()

    def last_copy(number):
        first, rows = ((0, 128), (128, 96), (224, 32), (0, 128), (128, 128))[number]
        part = pl.ds(first, rows)
        return remote(cross_out.at[part], cross_in.at[part], last_send.at[number], last_recv.at[number], peer)

    def send_last(number, batch, first, rows):
        begin = (0, 128, 224, 0, 128)[number]
        cross_out[begin : begin + rows, :] = reduced[reduced_rows(batch, first, rows), :].astype(BF16)
        last_copy(number).start()

    def vec_last():
        part = pl.ds(pl.multiple_of(8 - 8 * section, 8), 8)
        return remote(sums.at[0, part], sums.at[2 + RING, pl.ds(0, 8)], last_send.at[5], last_recv.at[5], peer)

    def nothing(point, t):
        pass

    def encoder_backward(run, source, grad, t, with_grads, with_store, at):
        m = run[1]

        @pl.when(t < TILES)
        def _():
            backward_out(run, grad, t, with_grads)

        at(0, t)

        @pl.when(t >= 1)
        def _():
            backward_taps(run, t - 1, with_grads)

        at(1, t)

        @pl.when(t >= 1)
        def _():
            done = t - 1

            def store(values):
                gio_stage[done % 2] = values

            backward_in(run, source, grad, done, with_grads, store if with_store else None)
            if with_store:
                gio_copy(m, done).start()
                settle(lambda s: gio_copy(m, s), done, TILES)

        at(2, t)

    def decoder_services(point, t):
        if point == 0:
            service(t, 0, (0, 1), (1, 1))
        else:
            for step in range(2, 6):
                service(t, step - 1, (point - 1, step))

    sentence_bounds(0)
    sentence_bounds(1)

    @pl.when(section == 0)
    def _():
        def spare_slot(t, half):
            return 8 * (t // 2) + 2 * (t % 2) + half

        def spare_copy(t, half):
            src = ends.at[0, tile_rows(t), pl.ds(half * H, H)]
            return pltpu.make_async_copy(src, red.at[spare_slot(t, half), pl.ds(0, TILE)], spare_sem.at[t, half])

        def read_spare(t, cols):
            halves = [red[spare_slot(t, half), 0:TILE, :] for half in range(2) if cols.start <= half * H < cols.stop]
            return jnp.concatenate(halves, axis=1)

        def park(j, back):
            src, dst = panels[2 + j], parked.at[j]
            return pltpu.make_async_copy(*((dst, src) if back else (src, dst)), park_sem.at[j])

        for t in range(TILES):
            for half in range(2):
                spare_copy(t, half).start()

        def encoder_forward(run, read, t, staged, at):
            m = run[1]

            @pl.when(t < TILES)
            def _():
                forward_in(run, read, t, LEAD)

            at(0, t)

            @pl.when(t >= 1)
            def _():
                done = t - 1

                def store(cols, values):
                    if staged:
                        act_stage[done % 2, :, cols] = values
                    else:
                        bufs[0, tile_rows(done), cols] = values

                forward_out(run, read, done, LEAD, store)
                act_copy(m, done, staged).start()
                settle(lambda s: act_copy(m, s, staged), done, TILES)

            at(1, t)

        def late_at(*plan):
            def at(point, t):
                for when, where, hop in plan:
                    if where == point:

                        @pl.when(t == when)
                        def _():
                            finish_early() if hop == 0 else advance_late(hop)

            return at

        early_run, decoder_run, late_run = (0, 1, 0, 0), (1, 1, 1, 1), (0, 0, 1, 2)

        @steps(TILES + 1, False)
        def _(t):
            encoder_forward(early_run, reader(own), t, False, late_at((0, 0, 0), (1, 0, 1), (3, 0, 2)))

        for t in range(TILES):
            act_pass(t).start()
        for t in range(TILES):
            for half in range(2):
                spare_copy(t, half).wait()

        @steps(TILES + 1, False)
        def _(t):
            encoder_forward(late_run, read_spare, t, True, late_at((0, 0, 3)))

        for j in range(2):
            park(j, False).start()
        advance_late(4)
        for j in range(2):
            park(j, False).wait()

        @steps(TILES + 1, False)
        def _(t):
            @pl.when(t < TILES)
            def _():
                wait_raw(t)
                forward_in(decoder_run, reader(bufs.at[0]), t, LEAD)
                forward_out(decoder_run, reader(bufs.at[0]), t, LEAD, None)
                backward_out(decoder_run, bufs.at[2], t, True)

            @pl.when(t >= 1)
            def _():
                done = t - 1

                def store(values):
                    bufs[2, tile_rows(done), :] = values

                backward_taps(decoder_run, done, True)
                backward_in(decoder_run, bufs.at[0], bufs.at[2], done, True, store)

        for j in range(2):
            park(j, True).start()
        begin_reduce(0)
        begin_reduce(1)

        @steps(TILES + 1, False)
        def _(t):
            encoder_backward(early_run, own, bufs.at[2], t, True, True, decoder_services)

        load_own(0).start()
        begin_reduce(2)
        begin_reduce(3)
        load_own(0).wait()
        for j in range(2):
            park(j, True).wait()

        def backward_services(point, t):
            if point == 0:
                service(t, 0, (2, 1), (3, 1))
            else:
                for when in range(1, 4):
                    service(t, when, (point + 1, when + 1))
                if point == 1:
                    service(t, 4, (2, 5))

        @steps(TILES + 1, False)
        def _(t):
            @pl.when(t < TILES)
            def _():
                grad_pass(t).wait_recv()

            encoder_backward(late_run, own, bufs.at[1], t, False, True, backward_services)

        reduce_step(3, 5)
        vec_step(5)
        for t in range(TILES):
            act_pass(t).wait_send()

    @pl.when(section == 1)
    def _():
        encoder_run, first_run, second_run = (0, 0, 0, 0), (1, 0, 1, 1), (1, 1, 1, 1)

        def decoder_forward(run, source, t, lead, at):
            def store(cols, values):
                act_stage[t % 2, :, cols] = values

            forward_in(run, reader(source), t, lead)
            at(0, t)
            forward_out(run, reader(source), t, lead, store)
            act_copy(run[1], t, True).start()
            settle(lambda s: act_copy(run[1], s, True), t, TILES)

        @steps(TILES + 2, False)
        def _(t):
            @pl.when(t < TILES)
            def _():
                wait_raw(t)
                forward_in(encoder_run, reader(bufs.at[2]), t, LEAD)

            @pl.when(t == 0)
            def _():
                finish_early()
                advance_late(1)

            @pl.when(t == 2)
            def _():
                advance_late(3)

            @pl.when((t >= 1) & (t <= TILES))
            def _():
                done = t - 1

                def store(cols, values):
                    bufs[0, tile_rows(done), cols] = values

                forward_out(encoder_run, reader(bufs.at[2]), done, LEAD, store)

            @pl.when(t == 1)
            def _():
                advance_late(2)

            @pl.when(t == 2)
            def _():
                advance_late(4)

            @steps(2, False)
            def _(second):
                @pl.when((t >= 2) & (t <= TILES) & ((second == 1) | (t == 2)))
                def _():
                    done = t - 2 + second
                    decoder_forward(first_run, bufs.at[0], done, LEAD - TILE, nothing)
                    backward_out(first_run, own, done, True)

            @pl.when(t >= 2)
            def _():
                done = t - 2

                def store(values):
                    gio_stage[done % 2] = values
                    own[tile_rows(done), :] = values

                backward_taps(first_run, done, True)
                backward_in(first_run, bufs.at[0], own, done, True, store)
                gio_copy(0, done).start()
                settle(lambda s: gio_copy(0, s), done, TILES)

                @pl.when(done >= 1)
                def _():
                    grad_pass(done - 1).start()

        grad_pass(TILES - 1).start()
        begin_reduce(0)
        begin_reduce(1)

        @steps(TILES + 1, False)
        def _(t):
            encoder_backward(encoder_run, bufs.at[2], own, t, True, False, decoder_services)

        load_own(1).start()
        begin_reduce(2)
        begin_reduce(3)
        load_own(1).wait()

        def encoder_services(point, t):
            if point == 0:
                service(t, 0, (2, 1), (3, 1))
                for when in range(1, 4):
                    service(t, when, (3, when + 1))
            elif point == 1:
                for when in range(0, 4):
                    service(t, when, (2, when + 2))
            else:
                service(t, 3, (3, 5))

        @steps(TILES + 1, False)
        def _(t):
            @pl.when(t < TILES)
            def _():
                act_pass(t).wait_recv()
                decoder_forward(second_run, bufs.at[1], t, LEAD, encoder_services)
                backward_out(second_run, own, t, False)

            encoder_services(1, t)

            @pl.when(t >= 1)
            def _():
                done = t - 1

                def store(values):
                    gio_stage[done % 2] = values

                backward_taps(second_run, done, False)
                backward_in(second_run, bufs.at[1], own, done, False, store)
                gio_copy(1, done).start()
                settle(lambda s: gio_copy(1, s), done, TILES)

            encoder_services(2, t)

        for t in range(TILES):
            grad_pass(t).wait_send()

    vec_share().wait_send()
    total = sums[2]
    for chip_sum in range(1, RING):
        total = total + sums[2 + chip_sum]
    sums[0] = total
    vec_last().start()

    for part in range(5):
        for hop in range(1, 5):
            for way in range(2):
                ring_copy(part, hop, way).wait_send()
        share_copy(part, ring, 0, core).wait_send()
        for slot in range(1, 8):
            share_copy(part, ring, slot, core).wait_send()
    for half in range(2):
        cross_copy(half, section).wait_send()
    for copy in cross_params(section):
        copy.wait_send()
    for number in range(2 * TILES):
        raw_copy(number).wait_send()


    @pl.when(section == 0)
    def _():
        last_copy(3).wait_recv()
        last_copy(4).wait_recv()
        terms = [reduced[reduced_rows(2), :], reduced[reduced_rows(3, 0, 128), :]]
        total = jnp.concatenate(terms, axis=0) + cross_in[...].astype(F32)
        grads_out[...] = jnp.concatenate([total[128:192], total[0:128], total[192:256]], axis=0)

    @pl.when(section == 1)
    def _():
        for number in range(3):
            last_copy(number).wait_recv()
        terms = [reduced[reduced_rows(0), :], reduced[reduced_rows(1), :], reduced[reduced_rows(3, 128, 32), :]]
        grads_out[...] = jnp.concatenate(terms, axis=0) + cross_in[...].astype(F32)

    vec_last().wait_recv()
    line = sums[0, pl.ds(pl.multiple_of(8 * section, 8), 8), :] + sums[2 + RING, 0:8, :]
    line_out[...] = line

    for way in range(2):
        for hop in range(1, 5 if way == 0 else 4):
            vec_copy(way, hop).wait_send()
    vec_last().wait_send()

    @pl.when(section == 0)
    def _():
        for number in range(3):
            last_copy(number).wait_send()

    @pl.when(section == 1)
    def _():
        for number in range(3, 5):
            last_copy(number).wait_send()


def finish_kernel(act, gio, grads, line, act_out, gio_out, in_out, out_out, tap_out, gain_out, bias_out, *scratch):
    act_buf, gio_buf, wide, grad_buf, in_buf, out_buf, tap_buf, sems, grad_sems = scratch
    count, rows = act_buf.shape[:2]

    def part(ref, i):
        return ref.at[pl.ds(i * rows, rows)]

    def gio_in(i):
        return pltpu.make_async_copy(part(gio, i), gio_buf.at[i], sems.at[0, i])

    def act_in(i):
        return pltpu.make_async_copy(part(act, i), act_buf.at[i], sems.at[1, i])

    def gio_back(i):
        return pltpu.make_async_copy(wide.at[i], part(gio_out, i), sems.at[2, i])

    def act_back(i):
        return pltpu.make_async_copy(act_buf.at[i], part(act_out, i), sems.at[3, i])

    grad_in = pltpu.make_async_copy(grads, grad_buf, grad_sems.at[0])
    backs = [
        pltpu.make_async_copy(src, dst, grad_sems.at[1 + j])
        for j, (src, dst) in enumerate(((in_buf, in_out), (out_buf, out_out), (tap_buf, tap_out)))
    ]
    gio_in(0).start()
    grad_in.start()
    for i in range(count):
        if i > 0:
            gio_in(i).start()
        act_in(i).start()
    grad_in.wait()
    for i in range(count):
        gio_in(i).wait()
        wide[i] = gio_buf[i].astype(F32)
        gio_back(i).start()
        act_in(i).wait()
        act_back(i).start()
    for j in range(PANELS):
        cols = slice(j * LANES, (j + 1) * LANES)
        in_buf[pl.ds(j, 64, PANELS), :] = grad_buf[0:64, cols]
        for half in range(2):
            first = 64 + 32 * half
            out_buf[pl.ds(PANELS * half + j, 32, 2 * PANELS), :] = grad_buf[first : first + 32, cols]
        for number, slot in enumerate((1, 2, 3, 0)):
            first = 128 + 32 * number
            tap_buf[pl.ds(4 * j + slot, 32, 4 * PANELS), :] = grad_buf[first : first + 32, cols]
    for back in backs:
        back.start()
    flat = jnp.concatenate([line[row : row + 1, :] for row in range(8)], axis=1)
    gain_out[...] = flat[:, 0 : 2 * D]
    bias_out[...] = flat[:, 2 * D : 5 * D]
    for i in range(count):
        act_back(i).wait()
        gio_back(i).wait()
    for back in backs:
        back.wait()


def finish(act, gio, grads, line):
    micro, rows = act.shape[:2]
    flat = (micro * rows, D)
    count = 4
    block = (count, micro * rows // count, D)
    shape = jax.ShapeDtypeStruct
    hbm = pl.BlockSpec(memory_space=pl.ANY)
    whole = pl.BlockSpec(memory_space=pltpu.VMEM)
    act, gio, grad_in, grad_out, grad_tap, gain_sum, bias_sum = pl.pallas_call(
        finish_kernel,
        out_shape=[
            shape(flat, BF16),
            shape(flat, F32),
            shape((64 * PANELS, LANES), F32),
            shape((64 * PANELS, LANES), F32),
            shape((128 * PANELS, LANES), F32),
            shape((1, 2 * D), F32),
            shape((1, 3 * D), F32),
        ],
        in_specs=[hbm, hbm, hbm, whole],
        out_specs=[hbm] * 5 + [whole] * 2,
        scratch_shapes=[
            pltpu.VMEM(block, BF16),
            pltpu.VMEM(block, BF16),
            pltpu.VMEM(block, F32),
            pltpu.VMEM((256, H), F32),
            pltpu.VMEM((64 * PANELS, LANES), F32),
            pltpu.VMEM((64 * PANELS, LANES), F32),
            pltpu.VMEM((128 * PANELS, LANES), F32),
            pltpu.SemaphoreType.DMA((4, count)),
            pltpu.SemaphoreType.DMA((4,)),
        ],
        compiler_params=pltpu.CompilerParams(vmem_limit_bytes=64 << 20),
        name="finish",
    )(act.reshape(flat), gio.reshape(flat), grads, line)
    grad_tap = grad_tap.reshape(32 * PANELS, 4, LANES).transpose(1, 0, 2).reshape(4, 32 * H)
    grads = (grad_in.reshape(1, 64 * H), grad_out.reshape(1, 64 * H), grad_tap)
    return (act.reshape(micro, rows, D), gio.reshape(micro, rows, D), *grads, gain_sum, bias_sum)


def local(group, block_ends, proj_in, proj_out, conv_taps, norm_gains, bias_terms, lengths, dilation):
    micro, rows = block_ends.shape[1:3]
    if group > 1:
        proj_in = lax.all_gather(proj_in, "lane", axis=1, tiled=True)
        proj_out = lax.all_gather(proj_out, "lane", axis=1, tiled=True)
        conv_taps = lax.all_gather(conv_taps, "lane", axis=2, tiled=True)
    vmem = pl.BlockSpec(memory_space=pltpu.VMEM)
    smem = pl.BlockSpec(memory_space=pltpu.SMEM)
    hbm = pl.BlockSpec(memory_space=pl.ANY)
    shape = jax.ShapeDtypeStruct
    dma = pltpu.SemaphoreType.DMA
    act, gio, grads, line, _ = pl.pallas_call(
        functools.partial(kernel, group),
        out_shape=[
            shape((micro, rows, D), BF16),
            shape((micro, rows, D), BF16),
            shape((256, H), F32),
            shape((8, 640), F32),
            shape((2, PANELS, LEN + 2 * PAD, LANES), F32),
        ],
        in_specs=[smem, smem, hbm, vmem, vmem, vmem, vmem, vmem],
        out_specs=[hbm, hbm, vmem, vmem, hbm],
        scratch_shapes=[
            pltpu.VMEM((2 * POSITIONS * PIECE, H), BF16),
            pltpu.VMEM((LEN, D), BF16),
            pltpu.VMEM((3, LEN, D), BF16),
            *[pltpu.VMEM((PANELS, LEN + 2 * PAD, LANES), F32) for _ in range(4)],
            pltpu.VMEM((PANELS, LEAD + LEN + PAD, LANES), F32),
            pltpu.VMEM((3, LEN, LANES), F32),
            pltpu.VMEM((2, LEN, LANES), jnp.int32),
            pltpu.VMEM((ACC_ROWS, H), F32),
            pltpu.VMEM((2, 3, 8, 2 * D), F32),
            pltpu.VMEM((2, TILE, D), BF16),
            pltpu.VMEM((2, TILE, D), BF16),
            pltpu.VMEM((2, 1, 2 * D), F32),
            pltpu.VMEM((2, 1, 3 * D), F32),
            pltpu.VMEM((3 + RING, 16, 640), F32),
            pltpu.VMEM((16, MOST, H), BF16),
            pltpu.VMEM((REDUCED, H), F32),
            pltpu.VMEM((256, H), BF16),
            pltpu.VMEM((256, H), BF16),
            pltpu.VMEM((PIECE, H), BF16),
            pltpu.VMEM((TILE, H), BF16),
            dma((2, 5, 4)),
            dma((2, 5, 4)),
            dma((5, 8)),
            dma((5, 8)),
            dma((4,)),
            dma((4,)),
            dma((2 * TILES,)),
            dma((2 * TILES,)),
            dma((TILES,)),
            dma((TILES,)),
            dma((5,)),
            dma((TILES, 2)),
            dma((2,)),
            dma((2,)),
            dma((2,)),
            dma((4, 2, 4)),
            dma((4, 2, 4)),
            dma((4, 5)),
            dma((4, 5)),
            dma((9,)),
            dma((9,)),
            dma((6,)),
            dma((6,)),
            pltpu.SemaphoreType.REGULAR((2,)),
        ],
        compiler_params=pltpu.CompilerParams(
            collective_id=0, has_side_effects=True, vmem_limit_bytes=64 << 20
        ),
        name="residual_blocks",
    )(dilation, lengths[:, 0, :], block_ends[0], proj_in, proj_out, conv_taps[0], norm_gains, bias_terms)
    act, gio, *grads, gain_sum, bias_sum = finish(act, gio, grads, line)
    grads[2] = grads[2][None]
    if group > 1:
        grads = tuple(
            lax.psum_scatter(part, "lane", scatter_dimension=part.ndim - 1, tiled=True) for part in grads
        )
        gain_sum, bias_sum = lax.psum((gain_sum, bias_sum), "lane")
    return (act[None], gio[None], *grads, gain_sum, bias_sum)


def solution(mesh):
    group = mesh.shape["dp"] // POSITIONS
    spread = "dp"
    if group > 1:
        mesh = Mesh(mesh.devices.reshape(2, POSITIONS, group), ("section", "dp", "lane"))
        spread = ("dp", "lane")
    placed = (
        P("section", None, spread, None),
        P("section", spread),
        P("section", spread),
        P("section", None, spread),
        P("section", None),
        P("section", None),
        P(None, spread, None),
        P(),
    )
    return jax.shard_map(
        functools.partial(local, group),
        mesh=mesh,
        in_specs=placed,
        out_specs=(
            P("section", None, spread, None),
            P("section", None, spread, None),
            P("section", spread),
            P("section", spread),
            P("section", None, spread),
            P("section", None),
            P("section", None),
        ),
        check_vma=False,
    )
```
